256 devices in a mesh: dp: 8 (over x, z_hi), ctx: 32 (over y, z_lo, core).
Axes of the slice: x: 4, y: 4, z: 8 (z_hi: 2, z_lo: 4; z = z_hi * 4 + z_lo), core: 2. Of those that a mesh axis runs over, the one named last changes fastest.
Arguments:
- layer_input: bfloat16 [8, 4096, 8192], P('dp', 'ctx'), may hold values from -6 to 6
- queries: bfloat16 [8, 4096, 1024], P('dp', 'ctx'), may hold values from -6 to 6
- keys: bfloat16 [8, 4096, 128], P('dp', 'ctx'), may hold values from -6 to 6
- values: bfloat16 [8, 4096, 128], P('dp', 'ctx'), may hold values from -6 to 6
- d_out: bfloat16 [8, 4096, 1024], P('dp', 'ctx'), may hold values from -6 to 6
- doc_lengths: int32 [8, 8], P('dp'), may hold values from 1 to 1024, 4096 in all within a row
- block_order: int32 [64], replicated, may hold values from 0 to 63, as said below
Outputs:
- query_grad: bfloat16 [8, 4096, 1024], P('dp', 'ctx')
- key_grad: bfloat16 [8, 4096, 128], P('dp', 'ctx')
- value_grad: bfloat16 [8, 4096, 128], P('dp', 'ctx')
- kv_weight_grad: float32 [32, 256, 256], P('ctx', 'dp')
The draws below stay inside these ranges and needn't reach their ends.
Inputs may be any that keep to these rules, and one draw needn't show every extreme that they name: `block_order`: entries 2r and 2r+1 are the blocks stored in rows 2r*64 to 2r*64 + 2*64 - 1; they sum to 63, and every block appears once.
All inputs are finite; a program needn't handle non-finite values.
Results may differ from the reference program's by a relative error of at most 0.012.
Values may be sent and summed in bfloat16 or wider, within the bound.
A program may use at most 64 MiB of HBM per device.

```python
import math
import jax
import jax.numpy as jnp
import numpy as np
from jax import lax

D = 8192
HD = 128
HEADS = 8
NDOCS = 8
HALF = 64
BLOCKS = 64
SEQ = 4096
SEQS = 8
N_CTX = 32


def draw_queries(key, part):
    first = jax.random.fold_in(jax.random.fold_in(key, 1), 0)
    result = jnp.clip(jax.random.normal(first, (SEQS, SEQ, HEADS, HD), jnp.float32), -6.0, 6.0)
    return result.reshape(SEQS, SEQ, HEADS * HD).astype(jnp.bfloat16)


def draw_keys(key, part):
    first = jax.random.fold_in(jax.random.fold_in(key, 2), 0)
    result = jnp.clip(jax.random.normal(first, (SEQS, SEQ, HD), jnp.float32), -6.0, 6.0)
    return result.astype(jnp.bfloat16)


def draw_block_order(key, part):
    first, second = jax.random.split(jax.random.fold_in(key, 3))
    count = BLOCKS // 2
    chosen = jax.random.permutation(first, count).astype(jnp.int32)
    flips = jax.random.randint(second, (count,), 0, 2)
    lower = jnp.where(flips == 1, BLOCKS - 1 - chosen, chosen).astype(jnp.int32)
    return jnp.stack([lower, BLOCKS - 1 - lower], axis=1).reshape(BLOCKS).astype(jnp.int32)


def block_levels(key, shape, cuts, least, largest):
    loudness = 1.0
    for position, blocks in cuts:
        draws = jax.random.uniform(jax.random.fold_in(jax.random.fold_in(key, 6), position), (blocks,), jnp.float32, least / len(cuts), largest / len(cuts))
        loudness = loudness * jnp.repeat(jnp.exp(draws), shape[position] // blocks).reshape((-1,) + (1,) * (len(shape) - 1 - position))
    return loudness


def length_profile(number_of, total, limit, slope):
    loads = [(1 << 20) // math.isqrt(standing ** slope) + 1 for standing in range(2, number_of + 1)]
    rest, given = total - limit - (number_of - 1), [1] * (number_of - 1)
    while rest > 0:
        candidates = [i for i in range(number_of - 1) if given[i] < limit]
        whole, remaining = sum([loads[i] for i in candidates]), rest
        for i in candidates:
            addition = min(limit - given[i], max(1, remaining * loads[i] // whole), rest)
            given[i] = given[i] + addition
            rest = rest - addition
    return np.array([limit] + given)


def uneven_parts(stream_key, amount, total, most, lean):
    if amount == 2:
        one = jax.random.randint(stream_key, (), max(1, total - most), min(most, total - 1) + 1)
        return jnp.stack([one, total - one])
    tallies = jnp.asarray(length_profile(amount, total, most, lean), jnp.int32)
    couples = (amount - 1) // 2
    giver, receiver = tallies[1:1 + 2 * couples:2], tallies[2:2 + 2 * couples:2]
    margin = jnp.minimum(giver - 1, most - receiver)
    passed = jax.random.randint(jax.random.fold_in(stream_key, 1), (couples,), 0, 1 << 20) % (margin + 1)
    tallies = tallies.at[1:1 + 2 * couples:2].set(giver - passed).at[2:2 + 2 * couples:2].set(receiver + passed)
    return tallies[jax.random.permutation(jax.random.fold_in(stream_key, 2), amount)]


def normal_values(rng, shape, deviation, most, cuts=(), kind=jnp.bfloat16):
    entries = deviation * jax.random.normal(rng, shape, jnp.float32)
    if cuts:
        entries = entries * block_levels(rng, shape, cuts, -0.22, 0.18)
    return jnp.clip(entries, -most, most).astype(kind)


def setup_inputs(seed: int = 0) -> dict:
    key_of = jax.random.split(jax.random.key(seed), 8)
    layer_input = normal_values(key_of[0], (SEQS, SEQ, D), 1.0, 6.0, ((0, 8), (1, 32)))
    queries = draw_queries(jax.random.fold_in(key_of[7], 71), 0)
    keys = draw_keys(jax.random.fold_in(key_of[7], 71), 0)
    values = normal_values(key_of[3], (SEQS, SEQ, HD), 1.0, 6.0, ((0, 8), (1, 32)))
    d_out = normal_values(key_of[4], (SEQS, SEQ, HEADS * HD), 1.0, 6.0, ((0, 8), (1, 32)))
    doc_lengths = jax.vmap(lambda own: uneven_parts(own, NDOCS, SEQ, SEQ // 4, 2))(jax.random.split(key_of[5], SEQS)).reshape((SEQS, NDOCS)).astype(jnp.int32)
    block_order = draw_block_order(jax.random.fold_in(key_of[7], 71), 0)
    return {"layer_input": layer_input, "queries": queries, "keys": keys, "values": values, "d_out": d_out, "doc_lengths": doc_lengths, "block_order": block_order}


def reference(layer_input, queries, keys, values, d_out, doc_lengths, block_order):
    scale = 1.0 / math.sqrt(HD)
    qblock = 512
    nblk = SEQ // qblock
    key_pos = (block_order[:, None] * HALF + jnp.arange(HALF, dtype=jnp.int32)[None, :]).reshape(SEQ).astype(jnp.int32)
    q_list = []
    k_list = []
    v_list = []
    weight = jnp.zeros((D, 2 * HD), jnp.float32)
    for seq in range(SEQS):
        ends = jnp.cumsum(doc_lengths[seq]).astype(jnp.int32)
        key_doc = lax.optimization_barrier(jnp.sum((key_pos[:, None] >= ends[None, :]).astype(jnp.int32), axis=1)).astype(jnp.int32)
        kfull = keys[seq].astype(jnp.float32)
        vfull = values[seq].astype(jnp.float32)
        qrows = queries[seq].astype(jnp.float32).reshape(nblk, qblock, HEADS, HD)
        drows = d_out[seq].astype(jnp.float32).reshape(nblk, qblock, HEADS, HD)
        qpos = key_pos.reshape(nblk, qblock)
        qdoc = key_doc.reshape(nblk, qblock)

        def step(carry, item):
            dk_sum, dv_sum = carry
            qb, db, pq, dq_doc = item
            mask = ((key_pos[None, :] <= pq[:, None]) & (key_doc[None, :] == dq_doc[:, None]))[None]
            s = jnp.einsum('thd,kd->htk', qb, kfull) * scale
            top = lax.optimization_barrier(jnp.max(jnp.where(mask, s, -1e+30), axis=2))
            total = lax.optimization_barrier(jnp.sum(jnp.where(mask, jnp.exp(s - top[..., None]), 0.0), axis=2))
            lse = top + jnp.log(total)
            p = jnp.where(mask, jnp.exp(s - lse[..., None]), 0.0)
            pb = lax.optimization_barrier(p.astype(jnp.bfloat16)).astype(jnp.float32)
            dprob = jnp.einsum('thd,kd->htk', db, vfull)
            delta = lax.optimization_barrier(jnp.sum(p * dprob, axis=2))
            ds = lax.optimization_barrier((p * (dprob - delta[..., None])).astype(jnp.bfloat16)).astype(jnp.float32)
            dq = (jnp.einsum('htk,kd->thd', ds, kfull) * scale).astype(jnp.bfloat16).reshape(qblock, HEADS * HD)
            dk_sum = dk_sum + jnp.einsum('htk,thd->kd', ds, qb)
            dv_sum = dv_sum + jnp.einsum('htk,thd->kd', pb, db)
            return ((dk_sum, dv_sum), dq)
        init = (jnp.zeros((SEQ, HD), jnp.float32), jnp.zeros((SEQ, HD), jnp.float32))
        (dk_sum, dv_sum), dq_blocks = lax.scan(step, init, (qrows, drows, qpos, qdoc))
        key_full = dk_sum * scale
        q_list.append(dq_blocks.reshape(SEQ, HEADS * HD))
        k_list.append(key_full.astype(jnp.bfloat16))
        v_list.append(dv_sum.astype(jnp.bfloat16))
        both = jnp.concatenate([key_full, dv_sum], axis=1)
        weight = weight + jnp.dot(layer_input[seq].astype(jnp.float32).T, both, preferred_element_type=jnp.float32, precision=lax.Precision.HIGHEST)
    weight = weight * (1.0 / math.sqrt(SEQS * SEQ))
    return (jnp.stack(q_list), jnp.stack(k_list), jnp.stack(v_list), weight.reshape(N_CTX, D // N_CTX, 2 * HD))
```

```python
import math

import jax
import jax.numpy as jnp
from jax import lax
from jax.experimental import pallas as pl
from jax.experimental.pallas import tpu as pltpu
from jax.sharding import PartitionSpec as P

NX, NY, NZL, NZH, NC = 4, 4, 4, 2, 2
NCTX = NY * NZL * NC
ROWS = 128
HD = 128
HEADS = 8
HALF = 64
BLOCKS = 64
SEQ = 4096
D = 8192
NDOCS = 8
XC = NX * NC
DCOLS = D // XC
CHUNK = 256
PER_CHUNK = CHUNK // HALF
MAX_CHUNKS = 5
QCOLS = HEADS * HALF
SCALE = 1.0 / math.sqrt(HD)
LOG2E = math.log2(math.e)
HIDDEN = -1e30
MESH = pl.DeviceIdType.MESH
F32 = jnp.float32
BF16 = jnp.bfloat16
NT = (((1,), (1,)), ((), ()))
TN = (((0,), (0,)), ((), ()))


def place():
    dp = lax.axis_index("dp")
    ctx = lax.axis_index("ctx")
    return dp // NZH, dp % NZH, ctx // (NZL * NC), (ctx // NC) % NZL, ctx % NC


def device(x, zh, y, zl, c):
    return (x * NZH + zh, (y * NZL + zl) * NC + c)


def remote(src, dst, send, recv, to):
    return pltpu.make_async_remote_copy(
        src_ref=src, dst_ref=dst, send_sem=send, recv_sem=recv, device_id=to, device_id_type=MESH
    )


def greet(peers):
    barrier = pltpu.get_barrier_semaphore()
    for peer in peers:
        pl.semaphore_signal(barrier, inc=1, device_id=peer, device_id_type=MESH)
    pl.semaphore_wait(barrier, len(peers))


def gather_kernel(k_ref, v_ref, x_hbm, kv_ref, xt_ref, xv, x_sem, zs, zr, ys, yr, cs, cr):
    x, zh, y, zl, c = place()

    def rank(q, p, core):
        return (((y - q + NY) % NY) * NZL + (zl - p + NZL) % NZL) * NC + core

    load_x = pltpu.make_async_copy(x_hbm.at[0], xv, x_sem)
    load_x.start()
    me = rank(0, 0, c)
    kv_ref[me, 0] = k_ref[0]
    kv_ref[me, 1] = v_ref[0]
    sibling = device(x, zh, y, zl, 1 - c)
    y_peers = [device(x, zh, (y + o) % NY, zl, c) for o in range(1, NY)]
    z_peers = [device(x, zh, y, (zl + o) % NZL, c) for o in range(1, NZL)]
    greet([sibling] + y_peers + z_peers)
    sends = []

    def go(r, send, recv, to):
        copy = remote(kv_ref.at[r], kv_ref.at[r], send, recv, to)
        copy.start()
        sends.append(copy)

    def arrived(r, send, recv, to):
        remote(kv_ref.at[r], kv_ref.at[r], send, recv, to).wait_recv()

    for o in (2, 1, 3):
        go(me, zs.at[o - 1], zr.at[o - 1], z_peers[o - 1])
    for o in (2, 1, 3):
        go(me, ys.at[0, o - 1], yr.at[0, o - 1], y_peers[o - 1])
    go(me, cs.at[0, 0], cr.at[0, 0], sibling)

    load_x.wait()
    to_row = lax.broadcasted_iota(jnp.int32, (256, 256), 0)
    from_row = lax.broadcasted_iota(jnp.int32, (256, 256), 1)
    group = to_row // 64
    source = (group % 2) * 128 + (group // 2) * 64 + to_row % 64
    pick = jnp.where(source == from_row, 1.0, 0.0).astype(BF16)
    for k in range(NY * NZL // 2):
        for core in range(NC):
            for xh in range(NX // 2):
                at = 2 * k * 512 + core * 256 + xh * 128
                pair = jnp.concatenate([xv[:, at : at + 128], xv[:, at + 512 : at + 640]], axis=1)
                turned = lax.dot_general(pick, pair, NT, preferred_element_type=F32).astype(BF16)
                xt_ref[(2 * xh) * NC + core, k * 128 : (k + 1) * 128, :] = turned[:128]
                xt_ref[(2 * xh + 1) * NC + core, k * 128 : (k + 1) * 128, :] = turned[128:]

    for p in (1, 3, 2):
        r = rank(0, p, c)
        arrived(r, zs.at[p - 1], zr.at[p - 1], z_peers[p - 1])
        for o in (2, 1, 3):
            go(r, ys.at[p, o - 1], yr.at[p, o - 1], y_peers[o - 1])
        go(r, cs.at[0, p], cr.at[0, p], sibling)
    for p in (0, 1, 3, 2):
        for q in (1, 3, 2):
            r = rank(q, p, c)
            arrived(r, ys.at[p, q - 1], yr.at[p, q - 1], y_peers[q - 1])
            go(r, cs.at[q, p], cr.at[q, p], sibling)
    for p in range(NZL):
        for q in range(NY):
            arrived(rank(q, p, 1 - c), cs.at[q, p], cr.at[q, p], sibling)
    for copy in sends:
        copy.wait_send()


def attend_kernel(doc_ref, order_ref, q_ref, d_ref, kv_ref, dq_ref, part_ref, stored, acc, s_buf, g_buf, q8, d8, dq_acc):
    _, _, y, zl, c = place()
    r = (y * NZL + zl) * NC + c

    def invert(j, carry):
        stored[order_ref[j]] = j
        return carry

    lax.fori_loop(0, BLOCKS, invert, 0)

    def clear(j, carry):
        acc[j] = jnp.zeros((2, HALF, HD), F32)
        return carry

    lax.fori_loop(0, BLOCKS, clear, 0)
    ends = []
    end = 0
    for i in range(NDOCS):
        end = end + doc_ref[0, i]
        ends.append(end)

    for half in range(2):
        block = order_ref[2 * r + half]
        first = 0
        for end in ends:
            first = jnp.where(end <= block * HALF, end, first)
        block0 = first // HALF
        chunks = (block - block0) // PER_CHUNK + 1
        for h in range(HEADS):
            q8[h * HALF : (h + 1) * HALF, :] = q_ref[0, half * HALF : (half + 1) * HALF, h * HD : (h + 1) * HD]
            d8[h * HALF : (h + 1) * HALF, :] = d_ref[0, half * HALF : (half + 1) * HALF, h * HD : (h + 1) * HD]
        lane = lax.broadcasted_iota(jnp.int32, (1, 128), 1)
        query_pos = block * HALF + lane % HALF
        query_start = jnp.zeros((1, 128), jnp.int32)
        for end in ends:
            query_start = jnp.where(end <= query_pos, end, query_start)

        def places(ch):
            return [stored[jnp.minimum(block0 + ch * PER_CHUNK + t, BLOCKS - 1)] for t in range(PER_CHUNK)]

        def chunk_of(js, which):
            return jnp.concatenate([kv_ref[j // 2, which, j % 2] for j in js], axis=0)

        def score(ch, top):
            js = places(ch)
            s = lax.dot_general(chunk_of(js, 0), q8[...], NT, preferred_element_type=F32)
            g_buf[ch] = lax.dot_general(chunk_of(js, 1), d8[...], NT, preferred_element_type=F32)
            key_pos = (block0 + ch * PER_CHUNK) * HALF + lax.broadcasted_iota(jnp.int32, (CHUNK, 128), 0)
            bias = jnp.where((key_pos >= query_start) & (key_pos <= query_pos), 0.0, HIDDEN)
            s = s * (SCALE * LOG2E) + jnp.concatenate([bias] * (QCOLS // 128), axis=1)
            s_buf[ch] = s
            return jnp.maximum(top, jnp.max(s.reshape(CHUNK // 8, 8, QCOLS), axis=0))

        top = lax.fori_loop(0, chunks, score, jnp.full((8, QCOLS), HIDDEN, F32))
        top = jnp.max(top, axis=0, keepdims=True)

        def weigh(ch, carry):
            total, dot = carry
            p = jnp.exp2(s_buf[ch] - top)
            s_buf[ch] = p
            total = total + jnp.sum(p.reshape(CHUNK // 8, 8, QCOLS), axis=0)
            dot = dot + jnp.sum((p * g_buf[ch]).reshape(CHUNK // 8, 8, QCOLS), axis=0)
            return total, dot

        zeros = jnp.zeros((8, QCOLS), F32)
        total, dot = lax.fori_loop(0, chunks, weigh, (zeros, zeros))
        inverse = 1.0 / jnp.sum(total, axis=0, keepdims=True)
        delta = jnp.sum(dot, axis=0, keepdims=True) * inverse
        dq_acc[...] = jnp.zeros((HD, QCOLS), F32)

        def grads(ch, carry):
            js = places(ch)
            p = s_buf[ch] * inverse
            ds = (p * (g_buf[ch] - delta)).astype(BF16)
            dk = jnp.dot(ds, q8[...], preferred_element_type=F32)
            dv = jnp.dot(p.astype(BF16), d8[...], preferred_element_type=F32)
            dq_acc[...] += lax.dot_general(chunk_of(js, 0), ds, TN, preferred_element_type=F32)
            for t, j in enumerate(js):
                acc[j, 0] += dk[t * HALF : (t + 1) * HALF]
                acc[j, 1] += dv[t * HALF : (t + 1) * HALF]
            return carry

        lax.fori_loop(0, chunks, grads, 0)
        dq = (dq_acc[...] * SCALE).T
        for h in range(HEADS):
            dq_ref[0, half * HALF : (half + 1) * HALF, h * HD : (h + 1) * HD] = dq[h * HALF : (h + 1) * HALF].astype(BF16)

    def write(i, carry):
        for part in range(2):
            rows = slice(part * HALF, (part + 1) * HALF)
            part_ref[i % NC, i // (NZL * NC), (i // NC) % NZL, 0, rows] = (acc[2 * i + part, 0] * SCALE).astype(BF16)
            part_ref[i % NC, i // (NZL * NC), (i // NC) % NZL, 1, rows] = acc[2 * i + part, 1].astype(BF16)
        return carry

    lax.fori_loop(0, NCTX, write, 0)


def reduce_kernel(
    part_ref, xt_ref, kg_ref, vg_ref, wg_ref,
    mine, theirs, y_in, z_out, z_in, g_buf, x_buf, p_out, p_in, w_acc, w_out, w_in,
    local, a_s, a_r, c_s, c_r, y_s, y_r, z_s, z_r, g_s, g_r, p_s, p_r, w_s, w_r,
):
    x, zh, y, zl, c = place()
    slot = x * NC + c
    zz = zh * NZL + zl
    sibling = device(x, zh, y, zl, 1 - c)

    def xc_device(t):
        return device(t // NC, zh, y, zl, t % NC)

    xc_to = [(slot + o) % XC for o in range(1, XC)]
    xc_from = [(slot - o + XC) % XC for o in range(1, XC)]
    xc_peers = [xc_device(t) for t in xc_to]
    y_to = [(y + o) % NY for o in range(1, NY)]
    y_peers = [device(x, zh, t, zl, c) for t in y_to]
    z_to = [(zl + o) % NZL for o in range(1, NZL)]
    z_peers = [device(x, zh, y, t, c) for t in z_to]
    zz_to = [(zz + o) % (NZH * NZL) for o in range(1, NZH * NZL)]
    zz_peers = [device(x, t // NZL, y, t % NZL, c) for t in zz_to]
    keep = pltpu.make_async_copy(part_ref.at[c], mine, local.at[0])
    keep.start()
    keep_x = pltpu.make_async_copy(xt_ref.at[slot], x_buf.at[slot], local.at[1])
    keep_x.start()
    greet(xc_peers + y_peers + zz_peers)
    sends = []

    def go(src, dst, send, recv, to):
        copy = remote(src, dst, send, recv, to)
        copy.start()
        sends.append(copy)

    y_order = [2, 1, 3, 0]
    for o in y_order:
        t = (y + o) % NY
        go(part_ref.at[1 - c, t], theirs.at[t], c_s.at[o], c_r.at[o], sibling)
    for o in (4, 2, 6, 3, 5, 1, 7):
        go(xt_ref.at[xc_to[o - 1]], x_buf.at[slot], a_s.at[o - 1], a_r.at[o - 1], xc_peers[o - 1])
    keep.wait()

    z_order = [2, 1, 3, 0]
    for o in y_order:
        t = (y + o) % NY
        remote(part_ref.at[1 - c, t], theirs.at[t], c_s.at[o], c_r.at[o], sibling).wait_recv()
        for oz in z_order:
            tz = (zl + oz) % NZL
            mine[t, tz] = (mine[t, tz].astype(F32) + theirs[t, tz].astype(F32)).astype(BF16)
            if o:
                go(mine.at[t, tz], y_in.at[o - 1, oz], y_s.at[o - 1, oz], y_r.at[o - 1, oz], y_peers[o - 1])

    own = None
    for oz in z_order:
        tz = (zl + oz) % NZL
        total = mine[y, tz].astype(F32)
        for o in (1, 3, 2):
            remote(mine.at[y, tz], y_in.at[o - 1, oz], y_s.at[o - 1, oz], y_r.at[o - 1, oz], y_peers[o - 1]).wait_recv()
            total = total + y_in[o - 1, oz].astype(F32)
        if oz:
            z_out[oz - 1] = total.astype(BF16)
            go(z_out.at[oz - 1], z_in.at[oz - 1], z_s.at[oz - 1], z_r.at[oz - 1], z_peers[oz - 1])
        else:
            own = total
    for oz in (1, 3, 2):
        remote(z_out.at[oz - 1], z_in.at[oz - 1], z_s.at[oz - 1], z_r.at[oz - 1], z_peers[oz - 1]).wait_recv()
        own = own + z_in[oz - 1].astype(F32)
    rounded = own.astype(BF16)
    g_buf[slot, :, :HD] = rounded[0]
    g_buf[slot, :, HD:] = rounded[1]
    for o in (4, 2, 6, 3, 5, 1, 7):
        go(g_buf.at[slot], g_buf.at[slot], g_s.at[o - 1], g_r.at[o - 1], xc_peers[o - 1])
    kg_ref[0] = rounded[0]
    vg_ref[0] = rounded[1]

    keep_x.wait()
    for o in (1, 7, 2, 3, 5, 6, 4):
        t = xc_from[o - 1]
        remote(xt_ref.at[t], x_buf.at[t], a_s.at[o - 1], a_r.at[o - 1], xc_peers[o - 1]).wait_recv()
    for o in (1, 7, 2, 3, 5, 6, 4):
        t = xc_from[o - 1]
        remote(g_buf.at[t], g_buf.at[t], g_s.at[o - 1], g_r.at[o - 1], xc_peers[o - 1]).wait_recv()
    grads = jnp.concatenate([g_buf[t] for t in range(XC)], axis=0)
    own = None
    for o in y_order:
        t = (y + o) % NY
        rows = pl.ds(pl.multiple_of(t * 256, 256), 256)
        left = jnp.concatenate([x_buf[i, rows, :] for i in range(XC)], axis=1)
        term = jnp.dot(left, grads, preferred_element_type=F32)
        if o:
            p_out[o - 1] = term.astype(BF16)
            go(p_out.at[o - 1], p_in.at[o - 1], p_s.at[o - 1], p_r.at[o - 1], y_peers[o - 1])
        else:
            own = term
    for o in (1, 3, 2):
        remote(p_out.at[o - 1], p_in.at[o - 1], p_s.at[o - 1], p_r.at[o - 1], y_peers[o - 1]).wait_recv()
        own = own + p_in[o - 1].astype(F32)
    w_acc[...] = own.reshape(NZL * NZH, 32, 2 * HD)
    w_out[...] = own.reshape(NZL * NZH, 32, 2 * HD).astype(BF16)
    for o in (4, 3, 5, 2, 6, 1, 7):
        t = zz_to[o - 1]
        go(w_out.at[(t % NZL) * NZH + t // NZL], w_in.at[o - 1], w_s.at[o - 1], w_r.at[o - 1], zz_peers[o - 1])
    total = w_acc[zl * NZH + zh]
    for o in (1, 7, 2, 6, 3, 5, 4):
        remote(w_out.at[0], w_in.at[o - 1], w_s.at[o - 1], w_r.at[o - 1], zz_peers[o - 1]).wait_recv()
        total = total + w_in[o - 1].astype(F32)
    wg_ref[0] = total * (1.0 / math.sqrt(8 * SEQ))
    for copy in sends:
        copy.wait_send()


def per_device(layer_input, queries, keys, values, d_out, doc_lengths, block_order):
    vmem = pl.BlockSpec(memory_space=pltpu.VMEM)
    smem = pl.BlockSpec(memory_space=pltpu.SMEM)
    hbm = pl.BlockSpec(memory_space=pl.ANY)
    dma = pltpu.SemaphoreType.DMA
    kv, xt = pl.pallas_call(
        gather_kernel,
        out_shape=(
            jax.ShapeDtypeStruct((NCTX, 2, ROWS, HD), BF16),
            jax.ShapeDtypeStruct((XC, DCOLS, ROWS), BF16),
        ),
        in_specs=[vmem, vmem, hbm],
        out_specs=(vmem, vmem),
        scratch_shapes=[
            pltpu.VMEM((ROWS, D), BF16),
            dma(()), dma((3,)), dma((3,)), dma((4, 3)), dma((4, 3)), dma((4, 4)), dma((4, 4)),
        ],
        compiler_params=pltpu.CompilerParams(collective_id=0, has_side_effects=True, vmem_limit_bytes=32 << 20),
        name="gather_kv",
    )(keys, values, layer_input)
    dq, part = pl.pallas_call(
        attend_kernel,
        out_shape=(
            jax.ShapeDtypeStruct((1, ROWS, HEADS * HD), BF16),
            jax.ShapeDtypeStruct((NC, NY, NZL, 2, ROWS, HD), BF16),
        ),
        in_specs=[smem, smem, vmem, vmem, vmem],
        out_specs=(vmem, vmem),
        scratch_shapes=[
            pltpu.SMEM((BLOCKS,), jnp.int32),
            pltpu.VMEM((BLOCKS, 2, HALF, HD), F32),
            pltpu.VMEM((MAX_CHUNKS, CHUNK, QCOLS), F32),
            pltpu.VMEM((MAX_CHUNKS, CHUNK, QCOLS), F32),
            pltpu.VMEM((QCOLS, HD), BF16),
            pltpu.VMEM((QCOLS, HD), BF16),
            pltpu.VMEM((HD, QCOLS), F32),
        ],
        compiler_params=pltpu.CompilerParams(vmem_limit_bytes=40 << 20),
        name="attend",
    )(doc_lengths, block_order, queries, d_out, kv.reshape(NCTX, 2, 2, HALF, HD))
    kg, vg, wg = pl.pallas_call(
        reduce_kernel,
        out_shape=(
            jax.ShapeDtypeStruct((1, ROWS, HD), BF16),
            jax.ShapeDtypeStruct((1, ROWS, HD), BF16),
            jax.ShapeDtypeStruct((1, 32, 2 * HD), F32),
        ),
        in_specs=[hbm, hbm],
        out_specs=(vmem, vmem, vmem),
        scratch_shapes=[
            pltpu.VMEM((NY, NZL, 2, ROWS, HD), BF16),
            pltpu.VMEM((NY, NZL, 2, ROWS, HD), BF16),
            pltpu.VMEM((NY - 1, NZL, 2, ROWS, HD), BF16),
            pltpu.VMEM((NZL - 1, 2, ROWS, HD), BF16),
            pltpu.VMEM((NZL - 1, 2, ROWS, HD), BF16),
            pltpu.VMEM((XC, ROWS, 2 * HD), BF16),
            pltpu.VMEM((XC, DCOLS, ROWS), BF16),
            pltpu.VMEM((NY - 1, 256, 2 * HD), BF16),
            pltpu.VMEM((NY - 1, 256, 2 * HD), BF16),
            pltpu.VMEM((NZL * NZH, 32, 2 * HD), F32),
            pltpu.VMEM((NZL * NZH, 32, 2 * HD), BF16),
            pltpu.VMEM((NZL * NZH - 1, 32, 2 * HD), BF16),
            dma((2,)),
            dma((7,)), dma((7,)), dma((4,)), dma((4,)), dma((3, 4)), dma((3, 4)), dma((3,)), dma((3,)),
            dma((7,)), dma((7,)), dma((3,)), dma((3,)), dma((7,)), dma((7,)),
        ],
        compiler_params=pltpu.CompilerParams(collective_id=1, has_side_effects=True, vmem_limit_bytes=32 << 20),
        name="reduce",
    )(part, xt)
    return dq, kg, vg, wg


def solution(mesh):
    rows = P("dp", "ctx", None)
    return jax.shard_map(
        per_device,
        mesh=mesh,
        in_specs=(rows, rows, rows, rows, rows, P("dp", None), P()),
        out_specs=(rows, rows, rows, P("ctx", "dp", None)),
        check_vma=False,
    )
```

```python
import math

import jax
import jax.numpy as jnp
from jax import lax
from jax.experimental import pallas as pl
from jax.experimental.pallas import tpu as pltpu
from jax.sharding import PartitionSpec as P

NX, NY, NZL, NZH, NC = 4, 4, 4, 2, 2
NCTX = NY * NZL * NC
ROWS = 128
HD = 128
HEADS = 8
HALF = 64
BLOCKS = 64
SEQ = 4096
D = 8192
NDOCS = 8
XC = NX * NC
DCOLS = D // XC
WINDOW = 17
STEP = 4
QCOLS = HEADS * HALF
SCALE = 1.0 / math.sqrt(HD)
LOG2E = math.log2(math.e)
HIDDEN = -1e30
MESH = pl.DeviceIdType.MESH
F32 = jnp.float32
BF16 = jnp.bfloat16
NT = (((1,), (1,)), ((), ()))
TN = (((0,), (0,)), ((), ()))


def place():
    dp = lax.axis_index("dp")
    ctx = lax.axis_index("ctx")
    return dp // NZH, dp % NZH, ctx // (NZL * NC), (ctx // NC) % NZL, ctx % NC


def device(x, zh, y, zl, c):
    return (x * NZH + zh, (y * NZL + zl) * NC + c)


def remote(src, dst, send, recv, to):
    return pltpu.make_async_remote_copy(
        src_ref=src, dst_ref=dst, send_sem=send, recv_sem=recv, device_id=to, device_id_type=MESH
    )


def greet(peers):
    barrier = pltpu.get_barrier_semaphore()
    for peer in peers:
        pl.semaphore_signal(barrier, inc=1, device_id=peer, device_id_type=MESH)
    pl.semaphore_wait(barrier, len(peers))


def kernel(
    doc_ref, order_ref, order_row, k_hbm, v_hbm, x_hbm, q_hbm, d_hbm, dq_ref, kg_ref, vg_ref, wg_ref,
    stored, stored_v, k_all, v_all, xv, xt, x_in, q_in, d_in, q8, d8, p_buf, g_buf, ds_buf, acc, part,
    theirs, y_in, z_out, z_in, g_all, p_out, p_in, w_acc, w_out, w_in, local,
    gz_s, gz_r, gy_s, gy_r, gc_s, gc_r, a_s, a_r, c_s, c_r, y_s, y_r, z_s, z_r, g_s, g_r, p_s, p_r, w_s, w_r,
):
    x, zh, y, zl, c = place()
    kv = (k_all, v_all)
    slot = x * NC + c
    zz = zh * NZL + zl

    def rank(q, p, core):
        return (((y - q + NY) % NY) * NZL + (zl - p + NZL) % NZL) * NC + core

    me = rank(0, 0, c)
    loads = [
        pltpu.make_async_copy(k_hbm.at[0, pl.ds(0, HALF)], kv[0].at[me, 0], local.at[0]),
        pltpu.make_async_copy(k_hbm.at[0, pl.ds(HALF, HALF)], kv[0].at[me, 1], local.at[1]),
        pltpu.make_async_copy(v_hbm.at[0, pl.ds(0, HALF)], kv[1].at[me, 0], local.at[2]),
        pltpu.make_async_copy(v_hbm.at[0, pl.ds(HALF, HALF)], kv[1].at[me, 1], local.at[3]),
        pltpu.make_async_copy(x_hbm.at[0], xv, local.at[4]),
        pltpu.make_async_copy(q_hbm.at[0], q_in, local.at[5]),
        pltpu.make_async_copy(d_hbm.at[0], d_in, local.at[6]),
    ]
    for load in loads:
        load.start()

    sibling = device(x, zh, y, zl, 1 - c)
    y_peers = [device(x, zh, (y + o) % NY, zl, c) for o in range(1, NY)]
    z_peers = [device(x, zh, y, (zl + o) % NZL, c) for o in range(1, NZL)]
    xc_to = [(slot + o) % XC for o in range(1, XC)]
    xc_from = [(slot - o + XC) % XC for o in range(1, XC)]
    xc_peers = [device(t // NC, zh, y, zl, t % NC) for t in xc_to]
    zz_to = [(zz + o) % (NZH * NZL) for o in range(1, NZH * NZL)]
    zz_peers = [device(x, t // NZL, y, t % NZL, c) for t in zz_to]
    greet(xc_peers + y_peers + zz_peers)
    sends = []

    def go(src, dst, send, recv, to):
        copy = remote(src, dst, send, recv, to)
        copy.start()
        sends.append(copy)

    def arrived(dst, send, recv, to):
        remote(dst, dst, send, recv, to).wait_recv()

    Y = (2, 1, 3)
    Z = (2, 1, 3)
    XS = (4, 2, 6, 3, 5, 1, 7)
    XR = (1, 7, 2, 3, 5, 6, 4)

    def to_z(w):
        for o in Z:
            go(kv[w].at[me], kv[w].at[me], gz_s.at[w, o - 1], gz_r.at[w, o - 1], z_peers[o - 1])

    def to_y(w, p):
        r = rank(0, p, c)
        for o in Y:
            go(kv[w].at[r], kv[w].at[r], gy_s.at[w, p, o - 1], gy_r.at[w, p, o - 1], y_peers[o - 1])

    def to_core(w, q, p):
        r = rank(q, p, c)
        go(kv[w].at[r], kv[w].at[r], gc_s.at[w, q, p], gc_r.at[w, q, p], sibling)

    def from_z(w, p):
        arrived(kv[w].at[rank(0, p, c)], gz_s.at[w, p - 1], gz_r.at[w, p - 1], z_peers[p - 1])

    def from_y(w, q, p):
        arrived(kv[w].at[rank(q, p, c)], gy_s.at[w, p, q - 1], gy_r.at[w, p, q - 1], y_peers[q - 1])

    def from_core(w):
        for p in range(NZL):
            for q in range(NY):
                arrived(kv[w].at[rank(q, p, 1 - c)], gc_s.at[w, q, p], gc_r.at[w, q, p], sibling)

    loads[0].wait()
    loads[1].wait()
    to_z(0)
    to_y(0, 0)
    to_core(0, 0, 0)
    loads[2].wait()
    loads[3].wait()
    to_z(1)
    to_core(1, 0, 0)

    same = order_row[...] == lax.broadcasted_iota(jnp.int32, (BLOCKS, BLOCKS), 0)
    column = lax.broadcasted_iota(jnp.int32, (BLOCKS, BLOCKS), 1)
    found = jnp.max(jnp.where(same, column, 0), axis=1, keepdims=True)
    stored_v[...] = jnp.broadcast_to(found, (BLOCKS, 128))
    load_stored = pltpu.make_async_copy(stored_v, stored, local.at[7])
    load_stored.start()

    to_row = lax.broadcasted_iota(jnp.int32, (256, 256), 0)
    from_row = lax.broadcasted_iota(jnp.int32, (256, 256), 1)
    group = to_row // 64
    source = (group % 2) * 128 + (group // 2) * 64 + to_row % 64
    pick = jnp.where(source == from_row, 1.0, 0.0).astype(BF16)

    def turn(core, xh):
        for k in range(NY * NZL // 2):
            at = 2 * k * 512 + core * 256 + xh * 128
            pair = jnp.concatenate([xv[:, at : at + 128], xv[:, at + 512 : at + 640]], axis=1)
            turned = lax.dot_general(pick, pair, NT, preferred_element_type=F32).astype(BF16)
            xt[(2 * xh) * NC + core, k * 128 : (k + 1) * 128, :] = turned[:128]
            xt[(2 * xh + 1) * NC + core, k * 128 : (k + 1) * 128, :] = turned[128:]

    loads[4].wait()
    turn(0, 0)
    for p in (1, 3, 2):
        from_z(0, p)
        to_y(0, p)
        to_core(0, 0, p)
    turn(0, 1)
    turn(1, 0)
    turn(1, 1)
    keep_x = pltpu.make_async_copy(xt.at[slot], x_in.at[slot], local.at[4])
    keep_x.start()
    for o in XS:
        go(xt.at[xc_to[o - 1]], x_in.at[slot], a_s.at[o - 1], a_r.at[o - 1], xc_peers[o - 1])
    to_y(1, 0)
    for p in (1, 3, 2):
        from_z(1, p)
        to_y(1, p)
        to_core(1, 0, p)
    for w in range(2):
        for half in range(2):
            acc[w, half, 0] = jnp.zeros((HALF, HD), F32)
            acc[w, half, WINDOW + 1] = jnp.zeros((HALF, HD), F32)
    loads[5].wait()
    loads[6].wait()
    for half in range(2):
        for h in range(HEADS):
            q8[half, h * HALF : (h + 1) * HALF, :] = q_in[half * HALF : (half + 1) * HALF, h * HD : (h + 1) * HD]
            d8[half, h * HALF : (h + 1) * HALF, :] = d_in[half * HALF : (half + 1) * HALF, h * HD : (h + 1) * HD]
    load_stored.wait()
    ends = []
    end = 0
    for i in range(NDOCS):
        end = end + doc_ref[0, i]
        ends.append(end)
    blocks = [order_ref[2 * me + half] for half in range(2)]
    for p in (0, 1, 3, 2):
        for q in (1, 3, 2):
            from_y(0, q, p)
            to_core(0, q, p)
    from_core(0)

    def each_step(step, carry):
        def body(i, carry):
            return step(i * STEP, STEP, pl.ds(pl.multiple_of(i * (STEP * HALF), STEP * HALF), STEP * HALF), carry)

        carry = lax.fori_loop(0, WINDOW // STEP, body, carry)
        return step(WINDOW - 1, 1, pl.ds((WINDOW - 1) * HALF, HALF), carry)

    def window(w, half, t, count):
        at = [jnp.clip(blocks[half] - (WINDOW - 1) + t + i, 0, BLOCKS - 1) for i in range(count)]
        js = [jnp.clip(stored[i, 0], 0, BLOCKS - 1) for i in at]
        return jnp.concatenate([kv[w][j // 2, j % 2] for j in js], axis=0)

    def fold(a):
        return a.reshape(a.shape[0] // 8, 8, QCOLS)

    def softmax(half):
        lane = lax.broadcasted_iota(jnp.int32, (1, 128), 1)
        query_pos = blocks[half] * HALF + lane % HALF
        query_start = jnp.zeros((1, 128), jnp.int32)
        for end in ends:
            query_start = jnp.where(end <= query_pos, end, query_start)

        def score(t, count, rows, top):
            s = lax.dot_general(window(0, half, t, count), q8[half], NT, preferred_element_type=F32)
            key_pos = (blocks[half] - (WINDOW - 1) + t) * HALF + lax.broadcasted_iota(jnp.int32, (count * HALF, 128), 0)
            bias = jnp.where((key_pos >= query_start) & (key_pos <= query_pos), 0.0, HIDDEN)
            s = s * (SCALE * LOG2E) + jnp.concatenate([bias] * (QCOLS // 128), axis=1)
            p_buf[half, rows] = s
            return jnp.maximum(top, jnp.max(fold(s), axis=0))

        top = each_step(score, jnp.full((8, QCOLS), HIDDEN, F32))
        top = jnp.max(top, axis=0, keepdims=True)

        def weigh(t, count, rows, total):
            p = jnp.exp2(p_buf[half, rows] - top)
            p_buf[half, rows] = p
            return total + jnp.sum(fold(p), axis=0)

        total = each_step(weigh, jnp.zeros((8, QCOLS), F32))
        inverse = 1.0 / jnp.sum(total, axis=0, keepdims=True)

        def value_terms(t, count, rows, carry):
            pb = (p_buf[half, rows] * inverse).astype(BF16)
            dv = jnp.dot(pb, d8[half], preferred_element_type=F32)
            acc[1, half, pl.ds(1 + t, count)] = dv.reshape(count, HALF, HD)
            return carry

        each_step(value_terms, 0)
        return inverse

    def key_terms(half, inverse):
        def prob_grads(t, count, rows, dot):
            g = lax.dot_general(window(1, half, t, count), d8[half], NT, preferred_element_type=F32)
            g_buf[rows] = g
            return dot + jnp.sum(fold(p_buf[half, rows] * g), axis=0)

        dot = each_step(prob_grads, jnp.zeros((8, QCOLS), F32))
        delta = jnp.sum(dot, axis=0, keepdims=True) * inverse

        def terms(t, count, rows, carry):
            ds = (p_buf[half, rows] * inverse * (g_buf[rows] - delta)).astype(BF16)
            ds_buf[half, rows] = ds
            dk = jnp.dot(ds, q8[half], preferred_element_type=F32) * SCALE
            acc[0, half, pl.ds(1 + t, count)] = dk.reshape(count, HALF, HD)
            return carry

        each_step(terms, 0)

    def query_terms(half):
        def terms(t, count, rows, total):
            return total + lax.dot_general(window(0, half, t, count), ds_buf[half, rows], TN, preferred_element_type=F32)

        dq = (each_step(terms, jnp.zeros((HD, QCOLS), F32)) * SCALE).T
        for h in range(HEADS):
            dq_ref[0, half * HALF : (half + 1) * HALF, h * HD : (h + 1) * HD] = dq[h * HALF : (h + 1) * HALF].astype(BF16)

    def in_stored_order(w, core, t):
        def body(i, carry):
            for part_half in range(2):
                block = order_ref[2 * ((t * NZL + i) * NC + core) + part_half]
                both = [acc[w, h, jnp.clip(block - blocks[h] + WINDOW, 0, WINDOW + 1)] for h in range(2)]
                part[w, core, t, i, part_half * HALF : (part_half + 1) * HALF] = (both[0] + both[1]).astype(BF16)
            return carry

        lax.fori_loop(0, NZL, body, 0)

    def sum_to_core(w):
        for o in (2, 1, 3, 0):
            t = (y + o) % NY
            in_stored_order(w, 1 - c, t)
            go(part.at[w, 1 - c, t], theirs.at[w, t], c_s.at[w, o], c_r.at[w, o], sibling)
        for o in (2, 1, 3, 0):
            in_stored_order(w, c, (y + o) % NY)

    def sum_to_y(w):
        for o in (2, 1, 3, 0):
            t = (y + o) % NY
            arrived(theirs.at[w, t], c_s.at[w, o], c_r.at[w, o], sibling)
            for oz in (2, 1, 3, 0):
                tz = (zl + oz) % NZL
                part[w, c, t, tz] = (part[w, c, t, tz].astype(F32) + theirs[w, t, tz].astype(F32)).astype(BF16)
                if o:
                    go(part.at[w, c, t, tz], y_in.at[w, o - 1, oz], y_s.at[w, o - 1, oz], y_r.at[w, o - 1, oz], y_peers[o - 1])

    def sum_to_z(w):
        for oz in (2, 1, 3, 0):
            total = part[w, c, y, (zl + oz) % NZL].astype(F32)
            for o in (1, 3, 2):
                arrived(y_in.at[w, o - 1, oz], y_s.at[w, o - 1, oz], y_r.at[w, o - 1, oz], y_peers[o - 1])
                total = total + y_in[w, o - 1, oz].astype(F32)
            if oz:
                z_out[w, oz - 1] = total.astype(BF16)
                go(z_out.at[w, oz - 1], z_in.at[w, oz - 1], z_s.at[w, oz - 1], z_r.at[w, oz - 1], z_peers[oz - 1])
        return total

    def sum_to_x(w, total, out_ref):
        for oz in (1, 3, 2):
            arrived(z_in.at[w, oz - 1], z_s.at[w, oz - 1], z_r.at[w, oz - 1], z_peers[oz - 1])
            total = total + z_in[w, oz - 1].astype(F32)
        rounded = total.astype(BF16)
        g_all[w, slot] = rounded
        for o in XS:
            go(g_all.at[w, slot], g_all.at[w, slot], g_s.at[w, o - 1], g_r.at[w, o - 1], xc_peers[o - 1])
        out_ref[0] = rounded

    def product(w):
        for o in XR:
            t = xc_from[o - 1]
            arrived(g_all.at[w, t], g_s.at[w, o - 1], g_r.at[w, o - 1], xc_peers[o - 1])
        right = jnp.concatenate([g_all[w, t] for t in range(XC)], axis=0)
        for o in (2, 1, 3, 0):
            rows = pl.ds(pl.multiple_of(((y + o) % NY) * 256, 256), 256)
            left = jnp.concatenate([x_in[i, rows, :] for i in range(XC)], axis=1)
            term = jnp.dot(left, right, preferred_element_type=F32)
            if o:
                p_out[w, o - 1] = term.astype(BF16)
                go(p_out.at[w, o - 1], p_in.at[w, o - 1], p_s.at[w, o - 1], p_r.at[w, o - 1], y_peers[o - 1])
        w_acc[w] = term.reshape(NZL * NZH, 32, HD)

    def product_to_z(w):
        for o in (1, 3, 2):
            arrived(p_in.at[w, o - 1], p_s.at[w, o - 1], p_r.at[w, o - 1], y_peers[o - 1])
        total = w_acc[w].reshape(256, HD) + p_in[w, 0].astype(F32) + p_in[w, 1].astype(F32) + p_in[w, 2].astype(F32)
        w_acc[w] = total.reshape(NZL * NZH, 32, HD)
        w_out[w] = total.reshape(NZL * NZH, 32, HD).astype(BF16)
        for o in (4, 3, 5, 2, 6, 1, 7):
            t = zz_to[o - 1]
            go(w_out.at[w, (t % NZL) * NZH + t // NZL], w_in.at[w, o - 1], w_s.at[w, o - 1], w_r.at[w, o - 1], zz_peers[o - 1])

    def finish(w):
        total = w_acc[w, zl * NZH + zh]
        for o in (1, 7, 2, 6, 3, 5, 4):
            arrived(w_in.at[w, o - 1], w_s.at[w, o - 1], w_r.at[w, o - 1], zz_peers[o - 1])
            total = total + w_in[w, o - 1].astype(F32)
        wg_ref[0, :, w * HD : (w + 1) * HD] = total * (1.0 / math.sqrt(8 * SEQ))

    inverses = [softmax(half) for half in range(2)]
    sum_to_core(1)
    for p in (0, 1, 3, 2):
        for q in (1, 3, 2):
            from_y(1, q, p)
            to_core(1, q, p)
    sum_to_y(1)
    from_core(1)
    for half in range(2):
        key_terms(half, inverses[half])
    sum_to_core(0)
    v_total = sum_to_z(1)
    sum_to_y(0)
    sum_to_x(1, v_total, vg_ref)
    for half in range(2):
        query_terms(half)
    k_total = sum_to_z(0)
    keep_x.wait()
    for o in XR:
        t = xc_from[o - 1]
        arrived(x_in.at[t], a_s.at[o - 1], a_r.at[o - 1], xc_peers[o - 1])
    product(1)
    sum_to_x(0, k_total, kg_ref)
    product_to_z(1)
    product(0)
    finish(1)
    product_to_z(0)
    finish(0)
    for copy in sends:
        copy.wait_send()


def per_device(layer_input, queries, keys, values, d_out, doc_lengths, block_order):
    vmem = pl.BlockSpec(memory_space=pltpu.VMEM)
    smem = pl.BlockSpec(memory_space=pltpu.SMEM)
    hbm = pl.BlockSpec(memory_space=pltpu.HBM)

    def dma(*shape):
        return [pltpu.SemaphoreType.DMA(shape)] * 2

    def buf(*shape, dtype=BF16):
        return pltpu.VMEM(shape, dtype)

    operands = (doc_lengths, block_order, block_order.reshape(1, BLOCKS), keys, values, layer_input, queries, d_out)
    dq, kg, vg, wg = pl.pallas_call(
        kernel,
        out_shape=(
            jax.ShapeDtypeStruct((1, ROWS, HEADS * HD), BF16),
            jax.ShapeDtypeStruct((1, ROWS, HD), BF16),
            jax.ShapeDtypeStruct((1, ROWS, HD), BF16),
            jax.ShapeDtypeStruct((1, 32, 2 * HD), F32),
        ),
        in_specs=[smem, smem, vmem, hbm, hbm, hbm, hbm, hbm],
        out_specs=(vmem, vmem, vmem, vmem),
        scratch_shapes=[
            pltpu.SMEM((BLOCKS, 128), jnp.int32),
            buf(BLOCKS, 128, dtype=jnp.int32),
            buf(NCTX, 2, HALF, HD),
            buf(NCTX, 2, HALF, HD),
            buf(ROWS, D),
            buf(XC, DCOLS, ROWS),
            buf(XC, DCOLS, ROWS),
            buf(ROWS, HEADS * HD),
            buf(ROWS, HEADS * HD),
            buf(2, QCOLS, HD),
            buf(2, QCOLS, HD),
            buf(2, WINDOW * HALF, QCOLS, dtype=F32),
            buf(WINDOW * HALF, QCOLS, dtype=F32),
            buf(2, WINDOW * HALF, QCOLS),
            buf(2, 2, WINDOW + 2, HALF, HD, dtype=F32),
            buf(2, NC, NY, NZL, ROWS, HD),
            buf(2, NY, NZL, ROWS, HD),
            buf(2, NY - 1, NZL, ROWS, HD),
            buf(2, NZL - 1, ROWS, HD),
            buf(2, NZL - 1, ROWS, HD),
            buf(2, XC, ROWS, HD),
            buf(2, NY - 1, 256, HD),
            buf(2, NY - 1, 256, HD),
            buf(2, NZL * NZH, 32, HD, dtype=F32),
            buf(2, NZL * NZH, 32, HD),
            buf(2, NZL * NZH - 1, 32, HD),
            pltpu.SemaphoreType.DMA((8,)),
            *dma(2, 3), *dma(2, 4, 3), *dma(2, 4, 4), *dma(7), *dma(2, 4), *dma(2, 3, 4), *dma(2, 3),
            *dma(2, 7), *dma(2, 3), *dma(2, 7),
        ],
        compiler_params=pltpu.CompilerParams(collective_id=0, has_side_effects=True, vmem_limit_bytes=48 << 20),
        name="backward",
    )(*(pltpu.with_memory_space_constraint(a, pltpu.HBM) for a in operands))
    return dq, kg, vg, wg


def solution(mesh):
    rows = P("dp", "ctx", None)
    return jax.shard_map(
        per_device,
        mesh=mesh,
        in_specs=(rows, rows, rows, rows, rows, P("dp", None), P()),
        out_specs=(rows, rows, rows, P("ctx", "dp", None)),
        check_vma=False,
    )
```

```python
import math

import jax
import jax.numpy as jnp
from jax import lax
from jax.experimental import pallas as pl
from jax.experimental.pallas import tpu as pltpu
from jax.sharding import PartitionSpec as P

NX, NY, NZL, NZH, NC = 4, 4, 4, 2, 2
NCTX = NY * NZL * NC
ROWS = 128
HD = 128
HEADS = 8
HALF = 64
BLOCKS = 64
SEQ = 4096
D = 8192
NDOCS = 8
XC = NX * NC
DCOLS = D // XC
WINDOW = 17
STEP = 4
QCOLS = HEADS * HALF
SCALE = 1.0 / math.sqrt(HD)
LOG2E = math.log2(math.e)
HIDDEN = -1e30
MESH = pl.DeviceIdType.MESH
F32 = jnp.float32
BF16 = jnp.bfloat16
NT = (((1,), (1,)), ((), ()))
TN = (((0,), (0,)), ((), ()))


def place():
    dp = lax.axis_index("dp")
    ctx = lax.axis_index("ctx")
    return dp // NZH, dp % NZH, ctx // (NZL * NC), (ctx // NC) % NZL, ctx % NC


def device(x, zh, y, zl, c):
    return (x * NZH + zh, (y * NZL + zl) * NC + c)


def remote(src, dst, send, recv, to):
    return pltpu.make_async_remote_copy(
        src_ref=src, dst_ref=dst, send_sem=send, recv_sem=recv, device_id=to, device_id_type=MESH
    )


def greet(peers):
    barrier = pltpu.get_barrier_semaphore()
    for peer in peers:
        pl.semaphore_signal(barrier, inc=1, device_id=peer, device_id_type=MESH)
    pl.semaphore_wait(barrier, len(peers))


def kernel(
    doc_ref, order_ref, order_row, k_hbm, v_hbm, x_hbm, q_hbm, d_hbm, dq_ref, kg_ref, vg_ref, wg_ref,
    stored, stored_v, k_all, v_all, xv, xt, x_in, q_in, d_in, q8, d8, p_buf, g_buf, ds_buf, acc, part,
    theirs, y_out, y_own, y_in, z_out, z_in, g_all, p_out, p_in, w_acc, w_out, w_in, local,
    gz_s, gz_r, gy_s, gy_r, gh_s, gh_r, gc_s, gc_r, a_s, a_r, c_s, c_r, y_s, y_r, z_s, z_r, g_s, g_r, gs_s, gs_r, p_s, p_r, w_s, w_r,
):
    x, zh, y, zl, c = place()
    kv = (k_all, v_all)
    slot = x * NC + c
    zz = zh * NZL + zl

    def rank(q, p, core):
        return (((y - q + NY) % NY) * NZL + (zl - p + NZL) % NZL) * NC + core

    me = rank(0, 0, c)
    loads = [
        pltpu.make_async_copy(k_hbm.at[0, pl.ds(0, HALF)], kv[0].at[me, 0], local.at[0]),
        pltpu.make_async_copy(k_hbm.at[0, pl.ds(HALF, HALF)], kv[0].at[me, 1], local.at[1]),
        pltpu.make_async_copy(v_hbm.at[0, pl.ds(0, HALF)], kv[1].at[me, 0], local.at[2]),
        pltpu.make_async_copy(v_hbm.at[0, pl.ds(HALF, HALF)], kv[1].at[me, 1], local.at[3]),
        pltpu.make_async_copy(x_hbm.at[0], xv, local.at[4]),
        pltpu.make_async_copy(q_hbm.at[0], q_in, local.at[5]),
        pltpu.make_async_copy(d_hbm.at[0], d_in, local.at[6]),
    ]
    for load in loads:
        load.start()

    sibling = device(x, zh, y, zl, 1 - c)
    y_peers = [device(x, zh, (y + o) % NY, zl, c) for o in range(1, NY)]
    z_peers = [device(x, zh, y, (zl + o) % NZL, c) for o in range(1, NZL)]
    xc_to = [(slot + o) % XC for o in range(1, XC)]
    xc_from = [(slot - o + XC) % XC for o in range(1, XC)]
    xc_peers = [device(t // NC, zh, y, zl, t % NC) for t in xc_to]
    x_peers = [device((x + o) % NX, zh, y, zl, c) for o in range(1, NX)]
    zz_to = [(zz + o) % (NZH * NZL) for o in range(1, NZH * NZL)]
    zz_peers = [device(x, t // NZL, y, t % NZL, c) for t in zz_to]
    greet(xc_peers + y_peers + zz_peers)
    sends = []

    def go(src, dst, send, recv, to):
        copy = remote(src, dst, send, recv, to)
        copy.start()
        sends.append(copy)

    def arrived(dst, send, recv, to):
        remote(dst, dst, send, recv, to).wait_recv()

    Z = (2, 1, 3)
    XS = (4, 2, 6, 3, 5, 1, 7)
    XR = (1, 7, 2, 3, 5, 6, 4)

    def to_z(w):
        for o in Z:
            go(kv[w].at[me], kv[w].at[me], gz_s.at[w, o - 1], gz_r.at[w, o - 1], z_peers[o - 1])

    def to_y(w, p):
        r = rank(0, p, c)
        for o in (1, 3):
            go(kv[w].at[r], kv[w].at[r], gy_s.at[w, p, o - 1], gy_r.at[w, p, o - 1], y_peers[o - 1])

    def relay(w, p):
        for q, half in ((1, 0), (3, 1)):
            r = rank(q, p, c)
            arrived(kv[w].at[r], gy_s.at[w, p, q - 1], gy_r.at[w, p, q - 1], y_peers[q - 1])
            go(kv[w].at[r, half], kv[w].at[r, half], gh_s.at[w, p, half], gh_r.at[w, p, half], y_peers[q - 1])
            to_core(w, q, p)

    def relayed(w, p):
        r = rank(2, p, c)
        for q, half in ((1, 0), (3, 1)):
            arrived(kv[w].at[r, half], gh_s.at[w, p, half], gh_r.at[w, p, half], y_peers[q - 1])
        to_core(w, 2, p)

    def to_core(w, q, p):
        r = rank(q, p, c)
        go(kv[w].at[r], kv[w].at[r], gc_s.at[w, q, p], gc_r.at[w, q, p], sibling)

    def from_z(w, p):
        arrived(kv[w].at[rank(0, p, c)], gz_s.at[w, p - 1], gz_r.at[w, p - 1], z_peers[p - 1])

    def from_core(w):
        for p in range(NZL):
            for q in range(NY):
                arrived(kv[w].at[rank(q, p, 1 - c)], gc_s.at[w, q, p], gc_r.at[w, q, p], sibling)

    loads[0].wait()
    loads[1].wait()
    to_z(0)
    to_y(0, 0)
    to_core(0, 0, 0)
    loads[2].wait()
    loads[3].wait()
    to_y(1, 0)
    to_core(1, 0, 0)

    same = order_row[...] == lax.broadcasted_iota(jnp.int32, (BLOCKS, BLOCKS), 0)
    column = lax.broadcasted_iota(jnp.int32, (BLOCKS, BLOCKS), 1)
    found = jnp.max(jnp.where(same, column, 0), axis=1, keepdims=True)
    stored_v[...] = jnp.broadcast_to(found, (BLOCKS, 128))
    load_stored = pltpu.make_async_copy(stored_v, stored, local.at[7])
    load_stored.start()

    to_row = lax.broadcasted_iota(jnp.int32, (256, 256), 0)
    from_row = lax.broadcasted_iota(jnp.int32, (256, 256), 1)
    group = to_row // 64
    source = (group % 2) * 128 + (group // 2) * 64 + to_row % 64
    pick = jnp.where(source == from_row, 1.0, 0.0).astype(BF16)

    def turn(core, xh):
        for k in range(NY * NZL // 2):
            at = 2 * k * 512 + core * 256 + xh * 128
            pair = jnp.concatenate([xv[:, at : at + 128], xv[:, at + 512 : at + 640]], axis=1)
            turned = lax.dot_general(pick, pair, NT, preferred_element_type=F32).astype(BF16)
            xt[(2 * xh) * NC + core, k * 128 : (k + 1) * 128, :] = turned[:128]
            xt[(2 * xh + 1) * NC + core, k * 128 : (k + 1) * 128, :] = turned[128:]

    loads[4].wait()
    turn(0, 0)
    turn(0, 1)
    to_z(1)
    for p in (1, 3, 2):
        from_z(0, p)
        to_y(0, p)
        to_core(0, 0, p)
    relay(0, 0)
    turn(1, 0)
    turn(1, 1)
    keep_x = pltpu.make_async_copy(xt.at[slot], x_in.at[slot], local.at[4])
    keep_x.start()
    for o in XS:
        go(xt.at[xc_to[o - 1]], x_in.at[slot], a_s.at[o - 1], a_r.at[o - 1], xc_peers[o - 1])
    for p in (1, 3, 2):
        relay(0, p)
    for p in (1, 3, 2):
        from_z(1, p)
        to_y(1, p)
        to_core(1, 0, p)
    relay(1, 0)
    for w in range(2):
        for half in range(2):
            acc[w, half, 0] = jnp.zeros((HALF, HD), F32)
            acc[w, half, WINDOW + 1] = jnp.zeros((HALF, HD), F32)
    loads[5].wait()
    loads[6].wait()
    for half in range(2):
        for h in range(HEADS):
            q8[half, h * HALF : (h + 1) * HALF, :] = q_in[half * HALF : (half + 1) * HALF, h * HD : (h + 1) * HD]
            d8[half, h * HALF : (h + 1) * HALF, :] = d_in[half * HALF : (half + 1) * HALF, h * HD : (h + 1) * HD]
    load_stored.wait()
    ends = []
    end = 0
    for i in range(NDOCS):
        end = end + doc_ref[0, i]
        ends.append(end)
    blocks = [order_ref[2 * me + half] for half in range(2)]
    for p in (0, 1, 3, 2):
        relayed(0, p)
    from_core(0)

    STEPS = [(t, min(STEP, WINDOW - t), slice(t * HALF, min(t + STEP, WINDOW) * HALF)) for t in range(0, WINDOW, STEP)]

    def window(w, half, t, count):
        at = [jnp.clip(blocks[half] - (WINDOW - 1) + t + i, 0, BLOCKS - 1) for i in range(count)]
        js = [jnp.clip(stored[i, 0], 0, BLOCKS - 1) for i in at]
        return jnp.concatenate([kv[w][j // 2, j % 2] for j in js], axis=0)

    def fold(a):
        return a.reshape(a.shape[0] // 8, 8, QCOLS)

    def query_span(half):
        query_pos = blocks[half] * HALF + lax.broadcasted_iota(jnp.int32, (1, 128), 1) % HALF
        query_start = jnp.zeros((1, 128), jnp.int32)
        for end in ends:
            query_start = jnp.where(end <= query_pos, end, query_start)
        return query_start, query_pos

    def scores():
        spans = [query_span(half) for half in range(2)]
        top = [jnp.full((8, QCOLS), HIDDEN, F32)] * 2
        for t, count, rows in STEPS:
            for half in range(2):
                s = lax.dot_general(window(0, half, t, count), q8[half], NT, preferred_element_type=F32)
                key_pos = (blocks[half] - (WINDOW - 1) + t) * HALF + lax.broadcasted_iota(jnp.int32, (count * HALF, 128), 0)
                bias = jnp.where((key_pos >= spans[half][0]) & (key_pos <= spans[half][1]), 0.0, HIDDEN)
                s = s * (SCALE * LOG2E) + jnp.concatenate([bias] * (QCOLS // 128), axis=1)
                p_buf[half, rows] = s
                top[half] = jnp.maximum(top[half], jnp.max(fold(s), axis=0))
        return [jnp.max(top[half], axis=0, keepdims=True) for half in range(2)]

    def weigh(top):
        total = [jnp.zeros((8, QCOLS), F32)] * 2
        for t, count, rows in STEPS:
            for half in range(2):
                p = jnp.exp2(p_buf[half, rows] - top[half])
                p_buf[half, rows] = p
                total[half] = total[half] + jnp.sum(fold(p), axis=0)
        return [1.0 / jnp.sum(total[half], axis=0, keepdims=True) for half in range(2)]

    def value_terms(inverse):
        for t, count, rows in STEPS:
            for half in range(2):
                pb = (p_buf[half, rows] * inverse[half]).astype(BF16)
                dv = jnp.dot(pb, d8[half], preferred_element_type=F32)
                acc[1, half, 1 + t : 1 + t + count] = dv.reshape(count, HALF, HD)

    def key_terms(inverse):
        dot = [jnp.zeros((8, QCOLS), F32)] * 2
        for t, count, rows in STEPS:
            for half in range(2):
                g = lax.dot_general(window(1, half, t, count), d8[half], NT, preferred_element_type=F32)
                g_buf[half, rows] = g
                dot[half] = dot[half] + jnp.sum(fold(p_buf[half, rows] * g), axis=0)
        delta = [jnp.sum(dot[half], axis=0, keepdims=True) * inverse[half] for half in range(2)]
        for t, count, rows in STEPS:
            for half in range(2):
                ds = (p_buf[half, rows] * inverse[half] * (g_buf[half, rows] - delta[half])).astype(BF16)
                ds_buf[half, rows] = ds
                dk = jnp.dot(ds, q8[half], preferred_element_type=F32) * SCALE
                acc[0, half, 1 + t : 1 + t + count] = dk.reshape(count, HALF, HD)

    def query_terms(half):
        total = jnp.zeros((HD, QCOLS), F32)
        for t, count, rows in STEPS:
            total = total + lax.dot_general(window(0, half, t, count), ds_buf[half, rows], TN, preferred_element_type=F32)
        dq = (total * SCALE).T
        for h in range(HEADS):
            dq_ref[0, half * HALF : (half + 1) * HALF, h * HD : (h + 1) * HD] = dq[h * HALF : (h + 1) * HALF].astype(BF16)

    def stored_half(w, r, part_half):
        block = order_ref[2 * r + part_half]
        both = [acc[w, h, jnp.clip(block - blocks[h] + WINDOW, 0, WINDOW + 1)] for h in range(2)]
        return both[0] + both[1]

    def sum_to_core(w):
        for oz in (2, 1, 3, 0):
            tz = (zl + oz) % NZL

            def body(i, carry):
                for part_half in range(2):
                    rows = slice(part_half * HALF, (part_half + 1) * HALF)
                    part[w, tz, i, rows] = stored_half(w, (i * NZL + tz) * NC + 1 - c, part_half).astype(BF16)
                return carry

            lax.fori_loop(0, NY, body, 0)
            go(part.at[w, tz], theirs.at[w, tz], c_s.at[w, oz], c_r.at[w, oz], sibling)

    def sum_to_y(w):
        for oz in (2, 1, 3, 0):
            tz = (zl + oz) % NZL
            arrived(theirs.at[w, tz], c_s.at[w, oz], c_r.at[w, oz], sibling)
            for o in (2, 1, 3, 0):
                t = (y + o) % NY
                for part_half in range(2):
                    rows = slice(part_half * HALF, (part_half + 1) * HALF)
                    total = stored_half(w, (t * NZL + tz) * NC + c, part_half) + theirs[w, tz, t, rows].astype(F32)
                    if o:
                        y_out[w, o - 1, oz, rows] = total.astype(BF16)
                    else:
                        y_own[w, oz, rows] = total
                if o:
                    go(y_out.at[w, o - 1, oz], y_in.at[w, o - 1, oz], y_s.at[w, o - 1, oz], y_r.at[w, o - 1, oz], y_peers[o - 1])

    def sum_to_z(w):
        for oz in (2, 1, 3, 0):
            total = y_own[w, oz]
            for o in (1, 3, 2):
                arrived(y_in.at[w, o - 1, oz], y_s.at[w, o - 1, oz], y_r.at[w, o - 1, oz], y_peers[o - 1])
                total = total + y_in[w, o - 1, oz].astype(F32)
            if oz:
                z_out[w, oz - 1] = total.astype(BF16)
                go(z_out.at[w, oz - 1], z_in.at[w, oz - 1], z_s.at[w, oz - 1], z_r.at[w, oz - 1], z_peers[oz - 1])
        return total

    def sum_to_x(w, total, out_ref):
        for oz in (1, 3, 2):
            arrived(z_in.at[w, oz - 1], z_s.at[w, oz - 1], z_r.at[w, oz - 1], z_peers[oz - 1])
            total = total + z_in[w, oz - 1].astype(F32)
        rounded = total.astype(BF16)
        g_all[w, slot] = rounded
        for o in (2, 1, 3):
            go(g_all.at[w, slot], g_all.at[w, slot], g_s.at[w, o - 1], g_r.at[w, o - 1], x_peers[o - 1])
        go(g_all.at[w, slot], g_all.at[w, slot], gs_s.at[w, 0], gs_r.at[w, 0], sibling)
        out_ref[0] = rounded

    def x_to_core(w):
        for o in (1, 3, 2):
            t = ((x - o + NX) % NX) * NC + c
            arrived(g_all.at[w, t], g_s.at[w, o - 1], g_r.at[w, o - 1], x_peers[o - 1])
            go(g_all.at[w, t], g_all.at[w, t], gs_s.at[w, o], gs_r.at[w, o], sibling)

    def product(w):
        for o in range(NX):
            arrived(g_all.at[w, ((x - o + NX) % NX) * NC + 1 - c], gs_s.at[w, o], gs_r.at[w, o], sibling)
        right = jnp.concatenate([g_all[w, t] for t in range(XC)], axis=0)
        for o in (2, 1, 3, 0):
            rows = pl.ds(pl.multiple_of(((y + o) % NY) * 256, 256), 256)
            left = jnp.concatenate([x_in[i, rows, :] for i in range(XC)], axis=1)
            term = jnp.dot(left, right, preferred_element_type=F32)
            if o:
                p_out[w, o - 1] = term.astype(BF16)
                go(p_out.at[w, o - 1], p_in.at[w, o - 1], p_s.at[w, o - 1], p_r.at[w, o - 1], y_peers[o - 1])
        w_acc[w] = term.reshape(NZL * NZH, 32, HD)

    def product_to_z(w):
        for o in (1, 3, 2):
            arrived(p_in.at[w, o - 1], p_s.at[w, o - 1], p_r.at[w, o - 1], y_peers[o - 1])
        total = w_acc[w].reshape(256, HD) + p_in[w, 0].astype(F32) + p_in[w, 1].astype(F32) + p_in[w, 2].astype(F32)
        w_acc[w] = total.reshape(NZL * NZH, 32, HD)
        w_out[w] = total.reshape(NZL * NZH, 32, HD).astype(BF16)
        for o in (4, 3, 5, 2, 6, 1, 7):
            t = zz_to[o - 1]
            go(w_out.at[w, (t % NZL) * NZH + t // NZL], w_in.at[w, o - 1], w_s.at[w, o - 1], w_r.at[w, o - 1], zz_peers[o - 1])

    def finish(w):
        total = w_acc[w, zl * NZH + zh]
        for o in (1, 7, 2, 6, 3, 5, 4):
            arrived(w_in.at[w, o - 1], w_s.at[w, o - 1], w_r.at[w, o - 1], zz_peers[o - 1])
            total = total + w_in[w, o - 1].astype(F32)
        wg_ref[0, :, w * HD : (w + 1) * HD] = total * (1.0 / math.sqrt(8 * SEQ))

    top = scores()
    for p in (1, 3, 2):
        relay(1, p)
    inverse = weigh(top)
    value_terms(inverse)
    sum_to_core(1)
    for p in (0, 1, 3, 2):
        relayed(1, p)
    sum_to_y(1)
    from_core(1)
    key_terms(inverse)
    sum_to_core(0)
    sum_to_y(0)
    v_total = sum_to_z(1)
    query_terms(0)
    sum_to_x(1, v_total, vg_ref)
    query_terms(1)
    x_to_core(1)
    k_total = sum_to_z(0)
    keep_x.wait()
    for o in XR:
        t = xc_from[o - 1]
        arrived(x_in.at[t], a_s.at[o - 1], a_r.at[o - 1], xc_peers[o - 1])
    product(1)
    sum_to_x(0, k_total, kg_ref)
    product_to_z(1)
    x_to_core(0)
    product(0)
    finish(1)
    product_to_z(0)
    finish(0)
    for copy in sends:
        copy.wait_send()


def write_kernel(*refs):
    sems = refs[-1]
    copies = [pltpu.make_async_copy(refs[i], refs[i + 4], sems.at[i]) for i in range(4)]
    for copy in copies:
        copy.start()
    for copy in copies:
        copy.wait()


def per_device(layer_input, queries, keys, values, d_out, doc_lengths, block_order):
    vmem = pl.BlockSpec(memory_space=pltpu.VMEM)
    smem = pl.BlockSpec(memory_space=pltpu.SMEM)
    hbm = pl.BlockSpec(memory_space=pltpu.HBM)

    def dma(*shape):
        return [pltpu.SemaphoreType.DMA(shape)] * 2

    def buf(*shape, dtype=BF16):
        return pltpu.VMEM(shape, dtype)

    operands = (doc_lengths, block_order, block_order.reshape(1, BLOCKS), keys, values, layer_input, queries, d_out)
    results = (
        jax.ShapeDtypeStruct((1, ROWS, HEADS * HD), BF16),
        jax.ShapeDtypeStruct((1, ROWS, HD), BF16),
        jax.ShapeDtypeStruct((1, ROWS, HD), BF16),
        jax.ShapeDtypeStruct((1, 32, 2 * HD), F32),
    )
    made = pl.pallas_call(
        kernel,
        out_shape=results,
        in_specs=[smem, smem, vmem, hbm, hbm, hbm, hbm, hbm],
        out_specs=(vmem, vmem, vmem, vmem),
        scratch_shapes=[
            pltpu.SMEM((BLOCKS, 128), jnp.int32),
            buf(BLOCKS, 128, dtype=jnp.int32),
            buf(NCTX, 2, HALF, HD),
            buf(NCTX, 2, HALF, HD),
            buf(ROWS, D),
            buf(XC, DCOLS, ROWS),
            buf(XC, DCOLS, ROWS),
            buf(ROWS, HEADS * HD),
            buf(ROWS, HEADS * HD),
            buf(2, QCOLS, HD),
            buf(2, QCOLS, HD),
            buf(2, WINDOW * HALF, QCOLS, dtype=F32),
            buf(2, WINDOW * HALF, QCOLS, dtype=F32),
            buf(2, WINDOW * HALF, QCOLS),
            buf(2, 2, WINDOW + 2, HALF, HD, dtype=F32),
            buf(2, NZL, NY, ROWS, HD),
            buf(2, NZL, NY, ROWS, HD),
            buf(2, NY - 1, NZL, ROWS, HD),
            buf(2, NZL, ROWS, HD, dtype=F32),
            buf(2, NY - 1, NZL, ROWS, HD),
            buf(2, NZL - 1, ROWS, HD),
            buf(2, NZL - 1, ROWS, HD),
            buf(2, XC, ROWS, HD),
            buf(2, NY - 1, 256, HD),
            buf(2, NY - 1, 256, HD),
            buf(2, NZL * NZH, 32, HD, dtype=F32),
            buf(2, NZL * NZH, 32, HD),
            buf(2, NZL * NZH - 1, 32, HD),
            pltpu.SemaphoreType.DMA((8,)),
            *dma(2, 3), *dma(2, 4, 3), *dma(2, 4, 2), *dma(2, 4, 4), *dma(7), *dma(2, 4), *dma(2, 3, 4), *dma(2, 3),
            *dma(2, 3), *dma(2, 4), *dma(2, 3), *dma(2, 7),
        ],
        compiler_params=pltpu.CompilerParams(collective_id=0, has_side_effects=True, vmem_limit_bytes=48 << 20),
        name="backward",
    )(*(pltpu.with_memory_space_constraint(a, pltpu.HBM) for a in operands))
    return pl.pallas_call(
        write_kernel,
        out_shape=results,
        in_specs=[vmem] * 4,
        out_specs=(hbm,) * 4,
        scratch_shapes=[pltpu.SemaphoreType.DMA((4,))],
        compiler_params=pltpu.CompilerParams(vmem_limit_bytes=4 << 20),
        name="write",
    )(*made)


def solution(mesh):
    rows = P("dp", "ctx", None)
    return jax.shard_map(
        per_device,
        mesh=mesh,
        in_specs=(rows, rows, rows, rows, rows, P("dp", None), P()),
        out_specs=(rows, rows, rows, P("ctx", "dp", None)),
        check_vma=False,
    )
```

```python
import math

import jax
import jax.numpy as jnp
from jax import lax
from jax.experimental import pallas as pl
from jax.experimental.pallas import tpu as pltpu
from jax.sharding import PartitionSpec as P

NX, NY, NZL, NZH, NC = 4, 4, 4, 2, 2
NCTX = NY * NZL * NC
ROWS = 128
HD = 128
HEADS = 8
HALF = 64
BLOCKS = 64
SEQ = 4096
D = 8192
NDOCS = 8
XC = NX * NC
DCOLS = D // XC
WINDOW = 17
STEP = 4
QCOLS = HEADS * HALF
SCALE = 1.0 / math.sqrt(HD)
LOG2E = math.log2(math.e)
HIDDEN = -1e30
MESH = pl.DeviceIdType.MESH
F32 = jnp.float32
BF16 = jnp.bfloat16
NT = (((1,), (1,)), ((), ()))
TN = (((0,), (0,)), ((), ()))


def place():
    dp = lax.axis_index("dp")
    ctx = lax.axis_index("ctx")
    return dp // NZH, dp % NZH, ctx // (NZL * NC), (ctx // NC) % NZL, ctx % NC


def device(x, zh, y, zl, c):
    return (x * NZH + zh, (y * NZL + zl) * NC + c)


def remote(src, dst, send, recv, to):
    return pltpu.make_async_remote_copy(
        src_ref=src, dst_ref=dst, send_sem=send, recv_sem=recv, device_id=to, device_id_type=MESH
    )


def kernel(
    doc_ref, order_ref, order_row, k_hbm, v_hbm, x_hbm, q_hbm, d_hbm, dq_ref, kg_ref, vg_ref, wg_ref,
    stored, stored_v, k_all, v_all, xv, xt, x_in, q_in, d_in, q8, d8, p_buf, g_buf, ds_buf, acc, part,
    theirs, y_out, y_own, y_in, z_out, z_in, g_all, p_out, p_in, w_acc, w_out, w_in, local,
    gz_s, gz_r, gy_s, gy_r, gc_s, gc_r, a_s, a_r, c_s, c_r, y_s, y_r, z_s, z_r, g_s, g_r, gs_s, gs_r, p_s, p_r, w_s, w_r,
):
    x, zh, y, zl, c = place()
    kv = (k_all, v_all)
    slot = x * NC + c
    zz = zh * NZL + zl

    def rank(q, p, core):
        return (((y - q + NY) % NY) * NZL + (zl - p + NZL) % NZL) * NC + core

    me = rank(0, 0, c)
    loads = [
        pltpu.make_async_copy(k_hbm.at[0, pl.ds(0, HALF)], kv[0].at[me, 0], local.at[0]),
        pltpu.make_async_copy(k_hbm.at[0, pl.ds(HALF, HALF)], kv[0].at[me, 1], local.at[1]),
        pltpu.make_async_copy(v_hbm.at[0, pl.ds(0, HALF)], kv[1].at[me, 0], local.at[2]),
        pltpu.make_async_copy(v_hbm.at[0, pl.ds(HALF, HALF)], kv[1].at[me, 1], local.at[3]),
        pltpu.make_async_copy(x_hbm.at[0], xv, local.at[4]),
        pltpu.make_async_copy(q_hbm.at[0], q_in, local.at[5]),
        pltpu.make_async_copy(d_hbm.at[0], d_in, local.at[6]),
    ]
    for load in loads:
        load.start()

    sibling = device(x, zh, y, zl, 1 - c)
    y_peers = [device(x, zh, (y + o) % NY, zl, c) for o in range(1, NY)]
    z_peers = [device(x, zh, y, (zl + o) % NZL, c) for o in range(1, NZL)]
    xc_to = [(slot + o) % XC for o in range(1, XC)]
    xc_from = [(slot - o + XC) % XC for o in range(1, XC)]
    xc_peers = [device(t // NC, zh, y, zl, t % NC) for t in xc_to]
    x_peers = [device((x + o) % NX, zh, y, zl, c) for o in range(1, NX)]
    zz_to = [(zz + o) % (NZH * NZL) for o in range(1, NZH * NZL)]
    zz_peers = [device(x, t // NZL, y, t % NZL, c) for t in zz_to]
    barrier = pltpu.get_barrier_semaphore()
    peers = xc_peers + y_peers + zz_peers
    for peer in peers:
        pl.semaphore_signal(barrier, inc=1, device_id=peer, device_id_type=MESH)

    to_row = lax.broadcasted_iota(jnp.int32, (256, 256), 0)
    from_row = lax.broadcasted_iota(jnp.int32, (256, 256), 1)
    group = to_row // 64
    source = (group % 2) * 128 + (group // 2) * 64 + to_row % 64
    pick = jnp.where(source == from_row, 1.0, 0.0).astype(BF16)

    def turn(core, xh):
        for k in range(NY * NZL // 2):
            at = 2 * k * 512 + core * 256 + xh * 128
            pair = jnp.concatenate([xv[:, at : at + 128], xv[:, at + 512 : at + 640]], axis=1)
            turned = lax.dot_general(pick, pair, NT, preferred_element_type=F32).astype(BF16)
            xt[(2 * xh) * NC + core, k * 128 : (k + 1) * 128, :] = turned[:128]
            xt[(2 * xh + 1) * NC + core, k * 128 : (k + 1) * 128, :] = turned[128:]

    loads[4].wait()
    turn(0, 0)
    turn(0, 1)
    pl.semaphore_wait(barrier, len(peers))
    sends = []

    def go(src, dst, send, recv, to):
        copy = remote(src, dst, send, recv, to)
        copy.start()
        sends.append(copy)

    def spread(t):
        at = (t - slot + XC) % XC - 1
        go(xt.at[t], x_in.at[slot], a_s.at[at], a_r.at[at], device(t // NC, zh, y, zl, t % NC))

    def arrived(dst, send, recv, to):
        remote(dst, dst, send, recv, to).wait_recv()

    Z = (2, 1, 3)
    XR = (1, 7, 2, 3, 5, 6, 4)

    def to_z(w):
        for o in Z:
            go(kv[w].at[me], kv[w].at[me], gz_s.at[w, o - 1], gz_r.at[w, o - 1], z_peers[o - 1])

    def to_y(w, p):
        r = rank(0, p, c)
        for o in (2, 1, 3):
            go(kv[w].at[r], kv[w].at[r], gy_s.at[w, p, o - 1], gy_r.at[w, p, o - 1], y_peers[o - 1])

    def from_y(w, p):
        for q in (1, 3, 2):
            r = rank(q, p, c)
            arrived(kv[w].at[r], gy_s.at[w, p, q - 1], gy_r.at[w, p, q - 1], y_peers[q - 1])
            to_core(w, q, p)

    def to_core(w, q, p):
        r = rank(q, p, c)
        go(kv[w].at[r], kv[w].at[r], gc_s.at[w, q, p], gc_r.at[w, q, p], sibling)

    def from_z(w, p):
        arrived(kv[w].at[rank(0, p, c)], gz_s.at[w, p - 1], gz_r.at[w, p - 1], z_peers[p - 1])

    def from_core(w):
        for p in range(NZL):
            for q in range(NY):
                arrived(kv[w].at[rank(q, p, 1 - c)], gc_s.at[w, q, p], gc_r.at[w, q, p], sibling)

    loads[0].wait()
    loads[1].wait()
    to_z(0)
    to_y(0, 0)
    to_core(0, 0, 0)
    loads[2].wait()
    loads[3].wait()

    same = order_row[...] == lax.broadcasted_iota(jnp.int32, (BLOCKS, BLOCKS), 0)
    column = lax.broadcasted_iota(jnp.int32, (BLOCKS, BLOCKS), 1)
    found = jnp.max(jnp.where(same, column, 0), axis=1, keepdims=True)
    stored_v[...] = jnp.broadcast_to(found, (BLOCKS, 128))
    load_stored = pltpu.make_async_copy(stored_v, stored, local.at[7])
    load_stored.start()

    for o in (2, 1, 3):
        spread((x + o) % NX * NC)
    for p in (1, 3, 2):
        from_z(0, p)
        to_y(0, p)
        to_core(0, 0, p)
    turn(1, 0)
    turn(1, 1)
    for o in (2, 1, 3):
        spread((x + o) % NX * NC + 1)
    spread(x * NC + 1 - c)
    keep_x = pltpu.make_async_copy(xt.at[slot], x_in.at[slot], local.at[4])
    keep_x.start()
    to_z(1)
    to_y(1, 0)
    to_core(1, 0, 0)
    for p in (1, 3, 2):
        from_z(1, p)
        to_y(1, p)
        to_core(1, 0, p)
    for w in range(2):
        for half in range(2):
            acc[w, half, 0] = jnp.zeros((HALF, HD), F32)
            acc[w, half, WINDOW + 1] = jnp.zeros((HALF, HD), F32)
    loads[5].wait()
    loads[6].wait()
    for half in range(2):
        for h in range(HEADS):
            q8[half, h * HALF : (h + 1) * HALF, :] = q_in[half * HALF : (half + 1) * HALF, h * HD : (h + 1) * HD]
            d8[half, h * HALF : (h + 1) * HALF, :] = d_in[half * HALF : (half + 1) * HALF, h * HD : (h + 1) * HD]
    load_stored.wait()
    ends = []
    end = 0
    for i in range(NDOCS):
        end = end + doc_ref[0, i]
        ends.append(end)
    blocks = [order_ref[2 * me + half] for half in range(2)]
    for p in (0, 1, 3, 2):
        from_y(0, p)
    from_core(0)

    STEPS = [(t, min(STEP, WINDOW - t), slice(t * HALF, min(t + STEP, WINDOW) * HALF)) for t in range(0, WINDOW, STEP)]

    def window(w, half, t, count):
        at = [jnp.clip(blocks[half] - (WINDOW - 1) + t + i, 0, BLOCKS - 1) for i in range(count)]
        js = [jnp.clip(stored[i, 0], 0, BLOCKS - 1) for i in at]
        return jnp.concatenate([kv[w][j // 2, j % 2] for j in js], axis=0)

    def fold(a):
        return a.reshape(a.shape[0] // 8, 8, QCOLS)

    def query_span(half):
        query_pos = blocks[half] * HALF + lax.broadcasted_iota(jnp.int32, (1, 128), 1) % HALF
        query_start = jnp.zeros((1, 128), jnp.int32)
        for end in ends:
            query_start = jnp.where(end <= query_pos, end, query_start)
        return query_start, query_pos

    def scores():
        spans = [query_span(half) for half in range(2)]
        top = [jnp.full((8, QCOLS), HIDDEN, F32)] * 2
        for t, count, rows in STEPS:
            for half in range(2):
                s = lax.dot_general(window(0, half, t, count), q8[half], NT, preferred_element_type=F32)
                key_pos = (blocks[half] - (WINDOW - 1) + t) * HALF + lax.broadcasted_iota(jnp.int32, (count * HALF, 128), 0)
                bias = jnp.where((key_pos >= spans[half][0]) & (key_pos <= spans[half][1]), 0.0, HIDDEN)
                s = s * (SCALE * LOG2E) + jnp.concatenate([bias] * (QCOLS // 128), axis=1)
                p_buf[half, rows] = s
                top[half] = jnp.maximum(top[half], jnp.max(fold(s), axis=0))
        return [jnp.max(top[half], axis=0, keepdims=True) for half in range(2)]

    def weigh(top):
        total = [jnp.zeros((8, QCOLS), F32)] * 2
        for t, count, rows in STEPS:
            for half in range(2):
                p = jnp.exp2(p_buf[half, rows] - top[half])
                p_buf[half, rows] = p
                total[half] = total[half] + jnp.sum(fold(p), axis=0)
        return [1.0 / jnp.sum(total[half], axis=0, keepdims=True) for half in range(2)]

    def value_terms(inverse):
        for t, count, rows in STEPS:
            for half in range(2):
                pb = (p_buf[half, rows] * inverse[half]).astype(BF16)
                dv = jnp.dot(pb, d8[half], preferred_element_type=F32)
                acc[1, half, 1 + t : 1 + t + count] = dv.reshape(count, HALF, HD)

    def key_terms(inverse):
        dot = [jnp.zeros((8, QCOLS), F32)] * 2
        for t, count, rows in STEPS:
            for half in range(2):
                g = lax.dot_general(window(1, half, t, count), d8[half], NT, preferred_element_type=F32)
                g_buf[half, rows] = g
                dot[half] = dot[half] + jnp.sum(fold(p_buf[half, rows] * g), axis=0)
        delta = [jnp.sum(dot[half], axis=0, keepdims=True) * inverse[half] for half in range(2)]
        for t, count, rows in STEPS:
            for half in range(2):
                ds = (p_buf[half, rows] * inverse[half] * (g_buf[half, rows] - delta[half])).astype(BF16)
                ds_buf[half, rows] = ds
                dk = jnp.dot(ds, q8[half], preferred_element_type=F32) * SCALE
                acc[0, half, 1 + t : 1 + t + count] = dk.reshape(count, HALF, HD)

    def query_terms(half):
        total = jnp.zeros((HD, QCOLS), F32)
        for t, count, rows in STEPS:
            total = total + lax.dot_general(window(0, half, t, count), ds_buf[half, rows], TN, preferred_element_type=F32)
        dq = (total * SCALE).T
        for h in range(HEADS):
            dq_ref[0, half * HALF : (half + 1) * HALF, h * HD : (h + 1) * HD] = dq[h * HALF : (h + 1) * HALF].astype(BF16)

    def stored_half(w, r, part_half):
        block = order_ref[2 * r + part_half]
        both = [acc[w, h, jnp.clip(block - blocks[h] + WINDOW, 0, WINDOW + 1)] for h in range(2)]
        return both[0] + both[1]

    def sum_to_core(w):
        for oz in (2, 1, 3, 0):
            tz = (zl + oz) % NZL

            def body(i, carry):
                for part_half in range(2):
                    rows = slice(part_half * HALF, (part_half + 1) * HALF)
                    part[w, tz, i, rows] = stored_half(w, (i * NZL + tz) * NC + 1 - c, part_half).astype(BF16)
                return carry

            lax.fori_loop(0, NY, body, 0)
            go(part.at[w, tz], theirs.at[w, tz], c_s.at[w, oz], c_r.at[w, oz], sibling)

    def sum_to_y(w):
        for oz in (2, 1, 3, 0):
            tz = (zl + oz) % NZL
            arrived(theirs.at[w, tz], c_s.at[w, oz], c_r.at[w, oz], sibling)
            for o in (2, 1, 3, 0):
                t = (y + o) % NY
                for part_half in range(2):
                    rows = slice(part_half * HALF, (part_half + 1) * HALF)
                    total = stored_half(w, (t * NZL + tz) * NC + c, part_half) + theirs[w, tz, t, rows].astype(F32)
                    if o:
                        y_out[w, o - 1, oz, rows] = total.astype(BF16)
                    else:
                        y_own[w, oz, rows] = total
                if o:
                    go(y_out.at[w, o - 1, oz], y_in.at[w, o - 1, oz], y_s.at[w, o - 1, oz], y_r.at[w, o - 1, oz], y_peers[o - 1])

    def sum_to_z(w):
        for oz in (2, 1, 3, 0):
            total = y_own[w, oz]
            for o in (1, 3, 2):
                arrived(y_in.at[w, o - 1, oz], y_s.at[w, o - 1, oz], y_r.at[w, o - 1, oz], y_peers[o - 1])
                total = total + y_in[w, o - 1, oz].astype(F32)
            if oz:
                z_out[w, oz - 1] = total.astype(BF16)
                go(z_out.at[w, oz - 1], z_in.at[w, oz - 1], z_s.at[w, oz - 1], z_r.at[w, oz - 1], z_peers[oz - 1])
        return total

    def sum_to_x(w, total, out_ref):
        for oz in (1, 3, 2):
            arrived(z_in.at[w, oz - 1], z_s.at[w, oz - 1], z_r.at[w, oz - 1], z_peers[oz - 1])
            total = total + z_in[w, oz - 1].astype(F32)
        rounded = total.astype(BF16)
        g_all[w, slot] = rounded
        for o in (2, 1, 3):
            go(g_all.at[w, slot], g_all.at[w, slot], g_s.at[w, o - 1], g_r.at[w, o - 1], x_peers[o - 1])
        go(g_all.at[w, slot], g_all.at[w, slot], gs_s.at[w, 0], gs_r.at[w, 0], sibling)
        out_ref[0] = rounded

    def x_to_core(w):
        for o in (1, 3, 2):
            t = ((x - o + NX) % NX) * NC + c
            arrived(g_all.at[w, t], g_s.at[w, o - 1], g_r.at[w, o - 1], x_peers[o - 1])
            go(g_all.at[w, t], g_all.at[w, t], gs_s.at[w, o], gs_r.at[w, o], sibling)

    def product(w):
        for o in range(NX):
            arrived(g_all.at[w, ((x - o + NX) % NX) * NC + 1 - c], gs_s.at[w, o], gs_r.at[w, o], sibling)
        right = jnp.concatenate([g_all[w, t] for t in range(XC)], axis=0)
        for o in (2, 1, 3, 0):
            rows = pl.ds(pl.multiple_of(((y + o) % NY) * 256, 256), 256)
            left = jnp.concatenate([x_in[i, rows, :] for i in range(XC)], axis=1)
            term = jnp.dot(left, right, preferred_element_type=F32)
            if o:
                p_out[w, o - 1] = term.astype(BF16)
                go(p_out.at[w, o - 1], p_in.at[w, o - 1], p_s.at[w, o - 1], p_r.at[w, o - 1], y_peers[o - 1])
        w_acc[w] = term.reshape(NZL * NZH, 32, HD)

    def product_to_z(w):
        for o in (1, 3, 2):
            arrived(p_in.at[w, o - 1], p_s.at[w, o - 1], p_r.at[w, o - 1], y_peers[o - 1])
        total = w_acc[w].reshape(256, HD) + p_in[w, 0].astype(F32) + p_in[w, 1].astype(F32) + p_in[w, 2].astype(F32)
        w_acc[w] = total.reshape(NZL * NZH, 32, HD)
        w_out[w] = total.reshape(NZL * NZH, 32, HD).astype(BF16)
        for o in (4, 3, 5, 2, 6, 1, 7):
            t = zz_to[o - 1]
            go(w_out.at[w, (t % NZL) * NZH + t // NZL], w_in.at[w, o - 1], w_s.at[w, o - 1], w_r.at[w, o - 1], zz_peers[o - 1])

    def finish(w):
        total = w_acc[w, zl * NZH + zh]
        for o in (1, 7, 2, 6, 3, 5, 4):
            arrived(w_in.at[w, o - 1], w_s.at[w, o - 1], w_r.at[w, o - 1], zz_peers[o - 1])
            total = total + w_in[w, o - 1].astype(F32)
        wg_ref[0, :, w * HD : (w + 1) * HD] = total * (1.0 / math.sqrt(8 * SEQ))

    top = scores()
    inverse = weigh(top)
    value_terms(inverse)
    sum_to_core(1)
    for p in (0, 1, 3, 2):
        from_y(1, p)
    sum_to_y(1)
    from_core(1)
    key_terms(inverse)
    sum_to_core(0)
    sum_to_y(0)
    v_total = sum_to_z(1)
    query_terms(0)
    sum_to_x(1, v_total, vg_ref)
    query_terms(1)
    x_to_core(1)
    k_total = sum_to_z(0)
    keep_x.wait()
    for o in XR:
        t = xc_from[o - 1]
        arrived(x_in.at[t], a_s.at[o - 1], a_r.at[o - 1], xc_peers[o - 1])
    product(1)
    sum_to_x(0, k_total, kg_ref)
    x_to_core(0)
    product(0)
    product_to_z(1)
    product_to_z(0)
    finish(1)
    finish(0)
    for copy in sends:
        copy.wait_send()


def write_kernel(*refs):
    sems = refs[-1]
    copies = [pltpu.make_async_copy(refs[i], refs[i + 4], sems.at[i]) for i in range(4)]
    for copy in copies:
        copy.start()
    for copy in copies:
        copy.wait()


def per_device(layer_input, queries, keys, values, d_out, doc_lengths, block_order):
    vmem = pl.BlockSpec(memory_space=pltpu.VMEM)
    smem = pl.BlockSpec(memory_space=pltpu.SMEM)
    hbm = pl.BlockSpec(memory_space=pltpu.HBM)

    def dma(*shape):
        return [pltpu.SemaphoreType.DMA(shape)] * 2

    def buf(*shape, dtype=BF16):
        return pltpu.VMEM(shape, dtype)

    operands = (doc_lengths, block_order, block_order.reshape(1, BLOCKS), keys, values, layer_input, queries, d_out)
    results = (
        jax.ShapeDtypeStruct((1, ROWS, HEADS * HD), BF16),
        jax.ShapeDtypeStruct((1, ROWS, HD), BF16),
        jax.ShapeDtypeStruct((1, ROWS, HD), BF16),
        jax.ShapeDtypeStruct((1, 32, 2 * HD), F32),
    )
    made = pl.pallas_call(
        kernel,
        out_shape=results,
        in_specs=[smem, smem, vmem, hbm, hbm, hbm, hbm, hbm],
        out_specs=(vmem, vmem, vmem, vmem),
        scratch_shapes=[
            pltpu.SMEM((BLOCKS, 128), jnp.int32),
            buf(BLOCKS, 128, dtype=jnp.int32),
            buf(NCTX, 2, HALF, HD),
            buf(NCTX, 2, HALF, HD),
            buf(ROWS, D),
            buf(XC, DCOLS, ROWS),
            buf(XC, DCOLS, ROWS),
            buf(ROWS, HEADS * HD),
            buf(ROWS, HEADS * HD),
            buf(2, QCOLS, HD),
            buf(2, QCOLS, HD),
            buf(2, WINDOW * HALF, QCOLS, dtype=F32),
            buf(2, WINDOW * HALF, QCOLS, dtype=F32),
            buf(2, WINDOW * HALF, QCOLS),
            buf(2, 2, WINDOW + 2, HALF, HD, dtype=F32),
            buf(2, NZL, NY, ROWS, HD),
            buf(2, NZL, NY, ROWS, HD),
            buf(2, NY - 1, NZL, ROWS, HD),
            buf(2, NZL, ROWS, HD, dtype=F32),
            buf(2, NY - 1, NZL, ROWS, HD),
            buf(2, NZL - 1, ROWS, HD),
            buf(2, NZL - 1, ROWS, HD),
            buf(2, XC, ROWS, HD),
            buf(2, NY - 1, 256, HD),
            buf(2, NY - 1, 256, HD),
            buf(2, NZL * NZH, 32, HD, dtype=F32),
            buf(2, NZL * NZH, 32, HD),
            buf(2, NZL * NZH - 1, 32, HD),
            pltpu.SemaphoreType.DMA((8,)),
            *dma(2, 3), *dma(2, 4, 3), *dma(2, 4, 4), *dma(7), *dma(2, 4), *dma(2, 3, 4), *dma(2, 3),
            *dma(2, 3), *dma(2, 4), *dma(2, 3), *dma(2, 7),
        ],
        compiler_params=pltpu.CompilerParams(collective_id=0, has_side_effects=True, vmem_limit_bytes=48 << 20),
        name="backward",
    )(*(pltpu.with_memory_space_constraint(a, pltpu.HBM) for a in operands))
    return pl.pallas_call(
        write_kernel,
        out_shape=results,
        in_specs=[vmem] * 4,
        out_specs=(hbm,) * 4,
        scratch_shapes=[pltpu.SemaphoreType.DMA((4,))],
        compiler_params=pltpu.CompilerParams(vmem_limit_bytes=4 << 20),
        name="write",
    )(*made)


def solution(mesh):
    rows = P("dp", "ctx", None)
    return jax.shard_map(
        per_device,
        mesh=mesh,
        in_specs=(rows, rows, rows, rows, rows, P("dp", None), P()),
        out_specs=(rows, rows, rows, P("ctx", "dp", None)),
        check_vma=False,
    )
```

```python
import math

import jax
import jax.numpy as jnp
from jax import lax
from jax.experimental import pallas as pl
from jax.experimental.pallas import tpu as pltpu
from jax.sharding import PartitionSpec as P

NX, NY, NZL, NZH, NC = 4, 4, 4, 2, 2
NCTX = NY * NZL * NC
ROWS = 128
HD = 128
HEADS = 8
HALF = 64
BLOCKS = 64
SEQ = 4096
D = 8192
NDOCS = 8
XC = NX * NC
DCOLS = D // XC
WINDOW = 17
STEP = 4
QCOLS = HEADS * HALF
SCALE = 1.0 / math.sqrt(HD)
LOG2E = math.log2(math.e)
HIDDEN = -1e30
MESH = pl.DeviceIdType.MESH
F32 = jnp.float32
BF16 = jnp.bfloat16
NT = (((1,), (1,)), ((), ()))
TN = (((0,), (0,)), ((), ()))


def place():
    dp = lax.axis_index("dp")
    ctx = lax.axis_index("ctx")
    return dp // NZH, dp % NZH, ctx // (NZL * NC), (ctx // NC) % NZL, ctx % NC


def device(x, zh, y, zl, c):
    return (x * NZH + zh, (y * NZL + zl) * NC + c)


def remote(src, dst, send, recv, to):
    return pltpu.make_async_remote_copy(
        src_ref=src, dst_ref=dst, send_sem=send, recv_sem=recv, device_id=to, device_id_type=MESH
    )


def kernel(
    doc_ref, order_ref, order_row, k_hbm, v_hbm, x_hbm, q_hbm, d_hbm, dq_ref, kg_ref, vg_ref, wg_ref,
    stored, stored_v, k_all, v_all, xv, xt, x_in, q_in, d_in, q8, d8, p_buf, g_buf, ds_buf, acc, part,
    theirs, y_out, y_own, y_in, z_out, z_in, g_all, p_out, p_in, w_acc, w_out, w_in, local,
    gz_s, gz_r, gy_s, gy_r, gc_s, gc_r, a_s, a_r, c_s, c_r, y_s, y_r, z_s, z_r, g_s, g_r, gs_s, gs_r, p_s, p_r, w_s, w_r,
):
    x, zh, y, zl, c = place()
    kv = (k_all, v_all)
    slot = x * NC + c
    zz = zh * NZL + zl

    def rank(q, p, core):
        return (((y - q + NY) % NY) * NZL + (zl - p + NZL) % NZL) * NC + core

    me = rank(0, 0, c)
    loads = [
        pltpu.make_async_copy(k_hbm.at[0, pl.ds(0, HALF)], kv[0].at[me, 0], local.at[0]),
        pltpu.make_async_copy(k_hbm.at[0, pl.ds(HALF, HALF)], kv[0].at[me, 1], local.at[1]),
        pltpu.make_async_copy(v_hbm.at[0, pl.ds(0, HALF)], kv[1].at[me, 0], local.at[2]),
        pltpu.make_async_copy(v_hbm.at[0, pl.ds(HALF, HALF)], kv[1].at[me, 1], local.at[3]),
        pltpu.make_async_copy(x_hbm.at[0], xv, local.at[4]),
        pltpu.make_async_copy(q_hbm.at[0], q_in, local.at[5]),
        pltpu.make_async_copy(d_hbm.at[0], d_in, local.at[6]),
    ]
    for load in loads:
        load.start()

    sibling = device(x, zh, y, zl, 1 - c)
    y_peers = [device(x, zh, (y + o) % NY, zl, c) for o in range(1, NY)]
    z_peers = [device(x, zh, y, (zl + o) % NZL, c) for o in range(1, NZL)]
    xc_to = [(slot + o) % XC for o in range(1, XC)]
    xc_from = [(slot - o + XC) % XC for o in range(1, XC)]
    xc_peers = [device(t // NC, zh, y, zl, t % NC) for t in xc_to]
    x_peers = [device((x + o) % NX, zh, y, zl, c) for o in range(1, NX)]
    zz_to = [(zz + o) % (NZH * NZL) for o in range(1, NZH * NZL)]
    zz_peers = [device(x, t // NZL, y, t % NZL, c) for t in zz_to]
    barrier = pltpu.get_barrier_semaphore()
    peers = xc_peers + y_peers + zz_peers
    for peer in peers:
        pl.semaphore_signal(barrier, inc=1, device_id=peer, device_id_type=MESH)

    to_row = lax.broadcasted_iota(jnp.int32, (256, 256), 0)
    from_row = lax.broadcasted_iota(jnp.int32, (256, 256), 1)
    group = to_row // 64
    source = (group % 2) * 128 + (group // 2) * 64 + to_row % 64
    pick = jnp.where(source == from_row, 1.0, 0.0).astype(BF16)

    def turn(core, xh):
        for k in range(NY * NZL // 2):
            at = 2 * k * 512 + core * 256 + xh * 128
            pair = jnp.concatenate([xv[:, at : at + 128], xv[:, at + 512 : at + 640]], axis=1)
            turned = lax.dot_general(pick, pair, NT, preferred_element_type=F32).astype(BF16)
            xt[(2 * xh) * NC + core, k * 128 : (k + 1) * 128, :] = turned[:128]
            xt[(2 * xh + 1) * NC + core, k * 128 : (k + 1) * 128, :] = turned[128:]

    loads[4].wait()
    turn(0, 0)
    turn(0, 1)
    pl.semaphore_wait(barrier, len(peers))
    sends = []

    def go(src, dst, send, recv, to):
        copy = remote(src, dst, send, recv, to)
        copy.start()
        sends.append(copy)

    def spread(t):
        at = (t - slot + XC) % XC - 1
        go(xt.at[t], x_in.at[slot], a_s.at[at], a_r.at[at], device(t // NC, zh, y, zl, t % NC))

    def arrived(dst, send, recv, to):
        remote(dst, dst, send, recv, to).wait_recv()

    Z = (2, 1, 3)
    XR = (1, 7, 2, 3, 5, 6, 4)

    def to_z(w):
        for o in Z:
            go(kv[w].at[me], kv[w].at[me], gz_s.at[w, o - 1], gz_r.at[w, o - 1], z_peers[o - 1])

    def to_y(w, p):
        r = rank(0, p, c)
        for o in (2, 1, 3):
            go(kv[w].at[r], kv[w].at[r], gy_s.at[w, p, o - 1], gy_r.at[w, p, o - 1], y_peers[o - 1])

    def from_y(w, p):
        for q in (1, 3, 2):
            r = rank(q, p, c)
            arrived(kv[w].at[r], gy_s.at[w, p, q - 1], gy_r.at[w, p, q - 1], y_peers[q - 1])
            to_core(w, q, p)

    def to_core(w, q, p):
        r = rank(q, p, c)
        go(kv[w].at[r], kv[w].at[r], gc_s.at[w, q, p], gc_r.at[w, q, p], sibling)

    def from_z(w, p):
        arrived(kv[w].at[rank(0, p, c)], gz_s.at[w, p - 1], gz_r.at[w, p - 1], z_peers[p - 1])

    def from_core(w):
        for p in range(NZL):
            for q in range(NY):
                arrived(kv[w].at[rank(q, p, 1 - c)], gc_s.at[w, q, p], gc_r.at[w, q, p], sibling)

    loads[0].wait()
    loads[1].wait()
    to_z(0)
    to_y(0, 0)
    to_core(0, 0, 0)
    loads[2].wait()
    loads[3].wait()

    same = order_row[...] == lax.broadcasted_iota(jnp.int32, (BLOCKS, BLOCKS), 0)
    column = lax.broadcasted_iota(jnp.int32, (BLOCKS, BLOCKS), 1)
    found = jnp.max(jnp.where(same, column, 0), axis=1, keepdims=True)
    stored_v[...] = jnp.broadcast_to(found, (BLOCKS, 128))
    load_stored = pltpu.make_async_copy(stored_v, stored, local.at[7])
    load_stored.start()

    for o in (2, 1, 3):
        spread((x + o) % NX * NC)
    for p in (1, 3, 2):
        from_z(0, p)
        to_y(0, p)
        to_core(0, 0, p)
    turn(1, 0)
    turn(1, 1)
    for o in (2, 1, 3):
        spread((x + o) % NX * NC + 1)
    spread(x * NC + 1 - c)
    keep_x = pltpu.make_async_copy(xt.at[slot], x_in.at[slot], local.at[4])
    keep_x.start()
    to_z(1)
    to_y(1, 0)
    to_core(1, 0, 0)
    for p in (1, 3, 2):
        from_z(1, p)
        to_y(1, p)
        to_core(1, 0, p)
    for w in range(2):
        for half in range(2):
            acc[w, half, 0] = jnp.zeros((HALF, HD), F32)
            acc[w, half, WINDOW + 1] = jnp.zeros((HALF, HD), F32)
    loads[5].wait()
    loads[6].wait()
    for half in range(2):
        for h in range(HEADS):
            q8[half, h * HALF : (h + 1) * HALF, :] = q_in[half * HALF : (half + 1) * HALF, h * HD : (h + 1) * HD]
            d8[half, h * HALF : (h + 1) * HALF, :] = d_in[half * HALF : (half + 1) * HALF, h * HD : (h + 1) * HD]
    load_stored.wait()
    ends = []
    end = 0
    for i in range(NDOCS):
        end = end + doc_ref[0, i]
        ends.append(end)
    blocks = [order_ref[2 * me + half] for half in range(2)]
    for p in (0, 1, 3, 2):
        from_y(0, p)
    from_core(0)

    STEPS = [(t, min(STEP, WINDOW - t), slice(t * HALF, min(t + STEP, WINDOW) * HALF)) for t in range(0, WINDOW, STEP)]

    def window(w, half, t, count):
        at = [jnp.clip(blocks[half] - (WINDOW - 1) + t + i, 0, BLOCKS - 1) for i in range(count)]
        js = [jnp.clip(stored[i, 0], 0, BLOCKS - 1) for i in at]
        return jnp.concatenate([kv[w][j // 2, j % 2] for j in js], axis=0)

    def fold(a):
        return a.reshape(a.shape[0] // 8, 8, QCOLS)

    def query_span(half):
        query_pos = blocks[half] * HALF + lax.broadcasted_iota(jnp.int32, (1, 128), 1) % HALF
        query_start = jnp.zeros((1, 128), jnp.int32)
        for end in ends:
            query_start = jnp.where(end <= query_pos, end, query_start)
        return query_start, query_pos

    def scores():
        spans = [query_span(half) for half in range(2)]
        top = [jnp.full((8, QCOLS), HIDDEN, F32)] * 2
        for t, count, rows in STEPS:
            for half in range(2):
                s = lax.dot_general(window(0, half, t, count), q8[half], NT, preferred_element_type=F32)
                key_pos = (blocks[half] - (WINDOW - 1) + t) * HALF + lax.broadcasted_iota(jnp.int32, (count * HALF, 128), 0)
                bias = jnp.where((key_pos >= spans[half][0]) & (key_pos <= spans[half][1]), 0.0, HIDDEN)
                s = s * (SCALE * LOG2E) + jnp.concatenate([bias] * (QCOLS // 128), axis=1)
                p_buf[half, rows] = s
                top[half] = jnp.maximum(top[half], jnp.max(fold(s), axis=0))
        return [jnp.max(top[half], axis=0, keepdims=True) for half in range(2)]

    def weigh(top):
        total = [jnp.zeros((8, QCOLS), F32)] * 2
        for t, count, rows in STEPS:
            for half in range(2):
                p = jnp.exp2(p_buf[half, rows] - top[half])
                p_buf[half, rows] = p
                total[half] = total[half] + jnp.sum(fold(p), axis=0)
        return [1.0 / jnp.sum(total[half], axis=0, keepdims=True) for half in range(2)]

    def value_terms(inverse):
        for t, count, rows in STEPS:
            for half in range(2):
                pb = (p_buf[half, rows] * inverse[half]).astype(BF16)
                dv = jnp.dot(pb, d8[half], preferred_element_type=F32)
                acc[1, half, 1 + t : 1 + t + count] = dv.reshape(count, HALF, HD)

    def key_terms(inverse):
        dot = [jnp.zeros((8, QCOLS), F32)] * 2
        for t, count, rows in STEPS:
            for half in range(2):
                g = lax.dot_general(window(1, half, t, count), d8[half], NT, preferred_element_type=F32)
                g_buf[half, rows] = g
                dot[half] = dot[half] + jnp.sum(fold(p_buf[half, rows] * g), axis=0)
        delta = [jnp.sum(dot[half], axis=0, keepdims=True) * inverse[half] for half in range(2)]
        for t, count, rows in STEPS:
            for half in range(2):
                ds = (p_buf[half, rows] * inverse[half] * (g_buf[half, rows] - delta[half])).astype(BF16)
                ds_buf[half, rows] = ds
                dk = jnp.dot(ds, q8[half], preferred_element_type=F32) * SCALE
                acc[0, half, 1 + t : 1 + t + count] = dk.reshape(count, HALF, HD)

    def query_terms(half):
        total = jnp.zeros((HD, QCOLS), F32)
        for t, count, rows in STEPS:
            total = total + lax.dot_general(window(0, half, t, count), ds_buf[half, rows], TN, preferred_element_type=F32)
        dq = (total * SCALE).T
        for h in range(HEADS):
            dq_ref[0, half * HALF : (half + 1) * HALF, h * HD : (h + 1) * HD] = dq[h * HALF : (h + 1) * HALF].astype(BF16)

    def stored_half(w, r, part_half):
        block = order_ref[2 * r + part_half]
        both = [acc[w, h, jnp.clip(block - blocks[h] + WINDOW, 0, WINDOW + 1)] for h in range(2)]
        return both[0] + both[1]

    def sum_to_core(w):
        for oz in (2, 1, 3, 0):
            tz = (zl + oz) % NZL

            def body(i, carry):
                for part_half in range(2):
                    rows = slice(part_half * HALF, (part_half + 1) * HALF)
                    part[w, tz, i, rows] = stored_half(w, (i * NZL + tz) * NC + 1 - c, part_half).astype(BF16)
                return carry

            lax.fori_loop(0, NY, body, 0)
            go(part.at[w, tz], theirs.at[w, tz], c_s.at[w, oz], c_r.at[w, oz], sibling)

    def sum_to_y(w):
        for oz in (2, 1, 3, 0):
            tz = (zl + oz) % NZL
            arrived(theirs.at[w, tz], c_s.at[w, oz], c_r.at[w, oz], sibling)
            for o in (2, 1, 3, 0):
                t = (y + o) % NY
                for part_half in range(2):
                    rows = slice(part_half * HALF, (part_half + 1) * HALF)
                    total = stored_half(w, (t * NZL + tz) * NC + c, part_half) + theirs[w, tz, t, rows].astype(F32)
                    if o:
                        y_out[w, o - 1, oz, rows] = total.astype(BF16)
                    else:
                        y_own[w, oz, rows] = total
                if o:
                    go(y_out.at[w, o - 1, oz], y_in.at[w, o - 1, oz], y_s.at[w, o - 1, oz], y_r.at[w, o - 1, oz], y_peers[o - 1])

    def sum_to_z(w):
        for oz in (2, 1, 3, 0):
            total = y_own[w, oz]
            for o in (1, 3, 2):
                arrived(y_in.at[w, o - 1, oz], y_s.at[w, o - 1, oz], y_r.at[w, o - 1, oz], y_peers[o - 1])
                total = total + y_in[w, o - 1, oz].astype(F32)
            if oz:
                z_out[w, oz - 1] = total.astype(BF16)
                go(z_out.at[w, oz - 1], z_in.at[w, oz - 1], z_s.at[w, oz - 1], z_r.at[w, oz - 1], z_peers[oz - 1])
        return total

    def sum_to_x(w, total, out_ref):
        for oz in (1, 3, 2):
            arrived(z_in.at[w, oz - 1], z_s.at[w, oz - 1], z_r.at[w, oz - 1], z_peers[oz - 1])
            total = total + z_in[w, oz - 1].astype(F32)
        rounded = total.astype(BF16)
        g_all[w, slot] = rounded
        for o in (2, 1, 3):
            go(g_all.at[w, slot], g_all.at[w, slot], g_s.at[w, o - 1], g_r.at[w, o - 1], x_peers[o - 1])
        go(g_all.at[w, slot], g_all.at[w, slot], gs_s.at[w, 0], gs_r.at[w, 0], sibling)
        out_ref[0] = rounded

    def x_to_core(w):
        for o in (1, 3, 2):
            t = ((x - o + NX) % NX) * NC + c
            arrived(g_all.at[w, t], g_s.at[w, o - 1], g_r.at[w, o - 1], x_peers[o - 1])
            go(g_all.at[w, t], g_all.at[w, t], gs_s.at[w, o], gs_r.at[w, o], sibling)

    def product(w):
        for o in range(NX):
            arrived(g_all.at[w, ((x - o + NX) % NX) * NC + 1 - c], gs_s.at[w, o], gs_r.at[w, o], sibling)
        right = jnp.concatenate([g_all[w, t] for t in range(XC)], axis=0)
        for o in (2, 1, 3, 0):
            rows = pl.ds(pl.multiple_of(((y + o) % NY) * 256, 256), 256)
            left = jnp.concatenate([x_in[i, rows, :] for i in range(XC)], axis=1)
            term = jnp.dot(left, right, preferred_element_type=F32)
            if o:
                p_out[w, o - 1] = term.astype(BF16)
                go(p_out.at[w, o - 1], p_in.at[w, o - 1], p_s.at[w, o - 1], p_r.at[w, o - 1], y_peers[o - 1])
        w_acc[w] = term.reshape(NZL * NZH, 32, HD)

    def product_to_z(w):
        for o in (1, 3, 2):
            arrived(p_in.at[w, o - 1], p_s.at[w, o - 1], p_r.at[w, o - 1], y_peers[o - 1])
        total = w_acc[w].reshape(256, HD) + p_in[w, 0].astype(F32) + p_in[w, 1].astype(F32) + p_in[w, 2].astype(F32)
        w_acc[w] = total.reshape(NZL * NZH, 32, HD)
        w_out[w] = total.reshape(NZL * NZH, 32, HD).astype(BF16)
        for o in (4, 3, 5, 2, 6, 1, 7):
            t = zz_to[o - 1]
            go(w_out.at[w, (t % NZL) * NZH + t // NZL], w_in.at[w, o - 1], w_s.at[w, o - 1], w_r.at[w, o - 1], zz_peers[o - 1])

    def finish(w):
        total = w_acc[w, zl * NZH + zh]
        for o in (1, 7, 2, 6, 3, 5, 4):
            arrived(w_in.at[w, o - 1], w_s.at[w, o - 1], w_r.at[w, o - 1], zz_peers[o - 1])
            total = total + w_in[w, o - 1].astype(F32)
        wg_ref[0, :, w * HD : (w + 1) * HD] = total * (1.0 / math.sqrt(8 * SEQ))

    top = scores()
    inverse = weigh(top)
    value_terms(inverse)
    sum_to_core(1)
    for p in (0, 1, 3, 2):
        from_y(1, p)
    sum_to_y(1)
    from_core(1)
    key_terms(inverse)
    sum_to_core(0)
    sum_to_y(0)
    v_total = sum_to_z(1)
    query_terms(0)
    sum_to_x(1, v_total, vg_ref)
    query_terms(1)
    k_total = sum_to_z(0)
    x_to_core(1)
    keep_x.wait()
    for o in XR:
        t = xc_from[o - 1]
        arrived(x_in.at[t], a_s.at[o - 1], a_r.at[o - 1], xc_peers[o - 1])
    product(1)
    sum_to_x(0, k_total, kg_ref)
    x_to_core(0)
    product(0)
    product_to_z(1)
    product_to_z(0)
    finish(1)
    finish(0)
    for copy in sends:
        copy.wait_send()


def write_kernel(*refs):
    sems = refs[-1]
    copies = [pltpu.make_async_copy(refs[i], refs[i + 4], sems.at[i]) for i in range(4)]
    for copy in copies:
        copy.start()
    for copy in copies:
        copy.wait()


def per_device(layer_input, queries, keys, values, d_out, doc_lengths, block_order):
    vmem = pl.BlockSpec(memory_space=pltpu.VMEM)
    smem = pl.BlockSpec(memory_space=pltpu.SMEM)
    hbm = pl.BlockSpec(memory_space=pltpu.HBM)

    def dma(*shape):
        return [pltpu.SemaphoreType.DMA(shape)] * 2

    def buf(*shape, dtype=BF16):
        return pltpu.VMEM(shape, dtype)

    operands = (doc_lengths, block_order, block_order.reshape(1, BLOCKS), keys, values, layer_input, queries, d_out)
    results = (
        jax.ShapeDtypeStruct((1, ROWS, HEADS * HD), BF16),
        jax.ShapeDtypeStruct((1, ROWS, HD), BF16),
        jax.ShapeDtypeStruct((1, ROWS, HD), BF16),
        jax.ShapeDtypeStruct((1, 32, 2 * HD), F32),
    )
    made = pl.pallas_call(
        kernel,
        out_shape=results,
        in_specs=[smem, smem, vmem, hbm, hbm, hbm, hbm, hbm],
        out_specs=(vmem, vmem, vmem, vmem),
        scratch_shapes=[
            pltpu.SMEM((BLOCKS, 128), jnp.int32),
            buf(BLOCKS, 128, dtype=jnp.int32),
            buf(NCTX, 2, HALF, HD),
            buf(NCTX, 2, HALF, HD),
            buf(ROWS, D),
            buf(XC, DCOLS, ROWS),
            buf(XC, DCOLS, ROWS),
            buf(ROWS, HEADS * HD),
            buf(ROWS, HEADS * HD),
            buf(2, QCOLS, HD),
            buf(2, QCOLS, HD),
            buf(2, WINDOW * HALF, QCOLS, dtype=F32),
            buf(2, WINDOW * HALF, QCOLS, dtype=F32),
            buf(2, WINDOW * HALF, QCOLS),
            buf(2, 2, WINDOW + 2, HALF, HD, dtype=F32),
            buf(2, NZL, NY, ROWS, HD),
            buf(2, NZL, NY, ROWS, HD),
            buf(2, NY - 1, NZL, ROWS, HD),
            buf(2, NZL, ROWS, HD, dtype=F32),
            buf(2, NY - 1, NZL, ROWS, HD),
            buf(2, NZL - 1, ROWS, HD),
            buf(2, NZL - 1, ROWS, HD),
            buf(2, XC, ROWS, HD),
            buf(2, NY - 1, 256, HD),
            buf(2, NY - 1, 256, HD),
            buf(2, NZL * NZH, 32, HD, dtype=F32),
            buf(2, NZL * NZH, 32, HD),
            buf(2, NZL * NZH - 1, 32, HD),
            pltpu.SemaphoreType.DMA((8,)),
            *dma(2, 3), *dma(2, 4, 3), *dma(2, 4, 4), *dma(7), *dma(2, 4), *dma(2, 3, 4), *dma(2, 3),
            *dma(2, 3), *dma(2, 4), *dma(2, 3), *dma(2, 7),
        ],
        compiler_params=pltpu.CompilerParams(collective_id=0, has_side_effects=True, vmem_limit_bytes=48 << 20),
        name="backward",
    )(*(pltpu.with_memory_space_constraint(a, pltpu.HBM) for a in operands))
    return pl.pallas_call(
        write_kernel,
        out_shape=results,
        in_specs=[vmem] * 4,
        out_specs=(hbm,) * 4,
        scratch_shapes=[pltpu.SemaphoreType.DMA((4,))],
        compiler_params=pltpu.CompilerParams(vmem_limit_bytes=4 << 20),
        name="write",
    )(*made)


def solution(mesh):
    rows = P("dp", "ctx", None)
    return jax.shard_map(
        per_device,
        mesh=mesh,
        in_specs=(rows, rows, rows, rows, rows, P("dp", None), P()),
        out_specs=(rows, rows, rows, P("ctx", "dp", None)),
        check_vma=False,
    )
```
